32 devices in a mesh: dp: 8 (over z, x), grp: 4 (over y, core).
Axes of the slice: x: 2, y: 2, z: 4, core: 2. Of those that a mesh axis runs over, the one named last changes fastest.
Arguments:
- embeddings: bfloat16 [1024, 64, 1024], P('dp', None, 'grp'), may hold values from -17 to 17
- lengths: int32 [1024], P('dp'), may hold values from 1 to 64
- parent_slot: int32 [1024], P('dp'), may hold values from 0 to 1023, as said below
- centroids: bfloat16 [1024, 16, 1024], P('dp', None, 'grp'), may hold values from -17 to 17
Outputs:
- refined: bfloat16 [1024, 16, 1024], P('dp', None, 'grp')
The draws below stay inside these ranges and needn't reach their ends.
Inputs may be any that keep to these rules, and one draw needn't show every extreme that they name: `parent_slot`: each parent has its own slot; slot // 128 is the index of dp that keeps that parent's centroids; the parents of one index of dp are kept by exactly 4 indices of dp, 32 by each. Rows past lengths[p] in a block are padding.
All inputs are finite; a program needn't handle non-finite values.
Results may differ from the reference program's by a relative error of at most 0.0057.
Values may be sent and summed in bfloat16 or wider, within the bound.
No kernel may reach another device: no remote copies, remote signals or barrier semaphores. Data moves between devices by JAX's collectives and lax.ppermute only.
A program may use at most 128 MiB of HBM per device.

```python
import math
import jax
import jax.numpy as jnp
from jax import lax

D = 1024
CHILDREN = 16
BLOCK = 64
ITERS = 2
PAR_DEV = 128
PARENTS = 1024
CAP = 32
N_DP = 8


def draw_scaled(key, shape):
    key_scale, key_core, key_column = jax.random.split(key, 3)
    width = shape[-1]
    position = jnp.arange(width, dtype=jnp.float32) / width
    jitter = jax.random.uniform(key_column, (width,), jnp.float32, 0.6, 1.4)
    column = jnp.exp(math.log(8.0) * (position - 1.0)) * jitter
    spread = jnp.exp(jax.random.uniform(key_scale, shape[:-1] + (1,), jnp.float32, math.log(0.3), math.log(3.0)))
    core = jnp.clip(jax.random.normal(key_core, shape, jnp.float32), -4.0, 4.0)
    return core * spread * column


def draw_embeddings(key, part):
    return draw_scaled(jax.random.fold_in(key, 11), (PARENTS, BLOCK, D)).astype(jnp.bfloat16)


def draw_centroids(key, part):
    return draw_scaled(jax.random.fold_in(key, 23), (PARENTS, CHILDREN, D)).astype(jnp.bfloat16)


def draw_parent_slot(key, part):
    key_shift, random_purpose_seed, key_local = jax.random.split(jax.random.fold_in(key, 37), 3)
    offsets = jnp.arange(N_DP, dtype=jnp.int32)
    forced = (offsets == 1) | (offsets == N_DP - 1) | (offsets == N_DP // 2)
    shift_score = jax.random.randint(key_shift, (N_DP,), 0, 1 << 20, dtype=jnp.int32)
    shift_score = jnp.where(forced, -1, shift_score) * N_DP + offsets
    shifts = jnp.argsort(shift_score)[:N_DP // 2].astype(jnp.int32)
    within_rank = jnp.arange(PAR_DEV, dtype=jnp.int32)[None, :]
    role_score = jax.random.randint(random_purpose_seed, (N_DP, PAR_DEV), 0, 1 << 16, dtype=jnp.int32) * PAR_DEV + within_rank
    role = jnp.argsort(role_score, axis=1).astype(jnp.int32)
    group = role // CAP
    inside_parent_position = role % CAP
    device = jnp.arange(N_DP, dtype=jnp.int32)[:, None]
    holder = (device + shifts[group]) % N_DP
    local_score = jax.random.randint(key_local, (N_DP, PAR_DEV), 0, 1 << 16, dtype=jnp.int32) * PAR_DEV + within_rank
    local_order = jnp.argsort(local_score, axis=1).astype(jnp.int32)
    local_slot = local_order[holder, group * CAP + inside_parent_position]
    return (holder * PAR_DEV + local_slot).reshape(-1).astype(jnp.int32)


def set_ends(result, rng, least, largest):
    shape = result.shape
    index_at = [jax.random.randint(jax.random.fold_in(rng, axis), (), 0, shape[axis]) for axis in range(len(shape))]
    result = result.at[tuple(index_at)].set(least)
    longest = shape.index(max(shape))
    index_at[longest] = (index_at[longest] + 1) % shape[longest]
    return result.at[tuple(index_at)].set(largest)


def setup_inputs(seed: int = 0) -> dict:
    key_list = jax.random.split(jax.random.key(seed), 5)
    embeddings = draw_embeddings(jax.random.fold_in(key_list[4], 71), 0)
    lengths = set_ends(jax.random.randint(key_list[1], (PARENTS,), 1, BLOCK + 1), jax.random.fold_in(key_list[1], 1), 1, BLOCK).astype(jnp.int32)
    parent_slot = draw_parent_slot(jax.random.fold_in(key_list[4], 71), 0)
    centroids = draw_centroids(jax.random.fold_in(key_list[4], 71), 0)
    return {"embeddings": embeddings, "lengths": lengths, "parent_slot": parent_slot, "centroids": centroids}


assignment_sharpness = 0.02
prior_weight = 1.0
epsilon = 1e-06

def refine_group(vectors, block_lengths, start):
    highest = lax.Precision.HIGHEST
    vec_f = vectors.astype(jnp.float32)
    sample_norm_multiplier = lax.rsqrt(lax.optimization_barrier(jnp.sum(vec_f * vec_f, axis=-1)) + epsilon)
    live_rows = jnp.arange(BLOCK)[None, :] < block_lengths[:, None]
    current = start
    for step in range(ITERS):
        cur_f = current.astype(jnp.float32)
        cluster_mean_norm_multiplier = lax.rsqrt(lax.optimization_barrier(jnp.sum(cur_f * cur_f, axis=-1)) + epsilon)
        cosine_similarity_matrix = jnp.einsum('pkd,pbd->pkb', cur_f, vec_f, precision=highest)
        membership_logits = cosine_similarity_matrix * cluster_mean_norm_multiplier[:, :, None] * sample_norm_multiplier[:, None, :] / assignment_sharpness
        raised = jnp.exp(membership_logits)
        weights = jnp.where(live_rows[:, None, :], raised / lax.optimization_barrier(jnp.sum(raised, axis=1, keepdims=True)), 0.0).astype(jnp.bfloat16)
        weight_f = weights.astype(jnp.float32)
        moments = jnp.einsum('pkb,pbd->pkd', weight_f, vec_f, precision=highest)
        totals = lax.optimization_barrier(jnp.sum(weight_f, axis=2))
        current = ((moments + prior_weight * cur_f) / (totals + prior_weight)[:, :, None]).astype(jnp.bfloat16)
    return current

def reference(embeddings, lengths, parent_slot, centroids):
    groups = PARENTS // PAR_DEV
    start = jnp.take(centroids, parent_slot, axis=0)
    grouped = (embeddings.reshape(groups, PAR_DEV, BLOCK, D), lengths.reshape(groups, PAR_DEV), start.reshape(groups, PAR_DEV, CHILDREN, D))
    updated_output = lax.map(lambda item: refine_group(item[0], item[1], item[2]), grouped)
    updated_output = updated_output.reshape(PARENTS, CHILDREN, D)
    return jnp.zeros_like(centroids).at[parent_slot].set(updated_output)
```

```python
import itertools
import jax
import jax.numpy as jnp
from jax import lax
from jax.sharding import PartitionSpec as P
from jax.experimental import pallas as pl
from jax.experimental.pallas import tpu as pltpu

F32, BF16, I32 = jnp.float32, jnp.bfloat16, jnp.int32
SHARPNESS = 0.02
PRIOR = 1.0
EPS = 1e-06
VMEM_BYTES = 40 * 1024 * 1024


def spec(space):
    return pl.BlockSpec(memory_space=space)


VM, SM, ANY = spec(pltpu.VMEM), spec(pltpu.SMEM), spec(pl.ANY)


def params():
    return pltpu.CompilerParams(vmem_limit_bytes=VMEM_BYTES)


def nt(a, b):
    return lax.dot_general(a, b, (((1,), (1,)), ((), ())), preferred_element_type=F32)


def sort_kernel(shift, peers, me_ref, slot_ref, len_ref, slot_out, perm_out, len_out):
    n = slot_ref.shape[1]
    row = lax.broadcasted_iota(I32, (n, n), 0)
    col = lax.broadcasted_iota(I32, (n, n), 1)
    slots = slot_ref[...]
    turn = (lax.shift_right_logical(slots, shift) - me_ref[0] + peers) & (peers - 1)
    key = (turn * n + lax.broadcasted_iota(I32, (1, n), 1)).astype(F32)
    diag = row == col

    def column(x):
        return jnp.sum(jnp.where(diag, jnp.broadcast_to(x, (n, n)), 0.0), axis=1, keepdims=True)

    keys = jnp.broadcast_to(key, (n, n))
    place = jnp.sum(jnp.where(keys < column(key), 1.0, 0.0), axis=1, keepdims=True)
    hit = jnp.broadcast_to(place, (n, n)).astype(I32) == col

    def sort(x_col):
        return jnp.sum(jnp.where(hit, x_col, 0.0), axis=0, keepdims=True).astype(I32)

    slot_out[...] = sort(column(slots.astype(F32)))
    perm_out[...] = sort(row.astype(F32))
    len_out[...] = sort(column(len_ref[...].astype(F32)))


def sort_parents(me, slots, lengths, peers):
    n = slots.shape[0]
    row = jax.ShapeDtypeStruct((1, n), I32)
    return pl.pallas_call(
        lambda *refs: sort_kernel(n.bit_length() - 1, peers, *refs),
        out_shape=(row, row, row),
        in_specs=[SM, VM, VM],
        out_specs=(VM, VM, VM),
        name="sort_parents",
    )(me, slots.reshape(1, n), lengths.reshape(1, n))


def split_kernel(core_ref, perm_ref, emb_ref, keep_ref, send_ref):
    count = keep_ref.shape[0]
    quarter = count // 2
    core = core_ref[0]
    for chunk in range(2):

        def move(r, carry, chunk=chunk):
            at = 2 * chunk * quarter + r
            send_ref[chunk * quarter + r] = emb_ref[perm_ref[0, at + (1 - core) * quarter]]
            keep_ref[chunk * quarter + r] = emb_ref[perm_ref[0, at + core * quarter]]
            return carry

        lax.fori_loop(0, quarter, move, 0, unroll=2)


def split_blocks(core, perm, emb):
    half = jax.ShapeDtypeStruct((emb.shape[0] // 2,) + emb.shape[1:], emb.dtype)
    return pl.pallas_call(
        split_kernel,
        out_shape=(half, half),
        in_specs=[SM, SM, VM],
        out_specs=(VM, VM),
        compiler_params=params(),
        cost_estimate=pl.CostEstimate(flops=0, bytes_accessed=2 * emb.size * 2, transcendentals=0),
        name="split_blocks",
    )(core, perm, emb)


def pack_kernel(peers, me_ref, table_ref, all_ref, cent_ref, o0, o1, o2, o3, list_ref, branch_ref):
    n = cent_ref.shape[0]
    quarter = n // 4
    shift = n.bit_length() - 1
    me = me_ref[0]

    def turn_of(q, i):
        return (lax.shift_right_logical(all_ref[q, i * quarter], shift) - (me ^ q) + peers) & (peers - 1)

    turns = [turn_of(0, i) for i in range(4)]
    bad = jnp.int32(0)
    for q in range(1, peers):
        for i in range(4):
            bad = bad | (turn_of(q, i) ^ turns[i])
    for half in range(2):
        at = turns[2 * half] * peers + turns[2 * half + 1]
        branch_ref[half] = jnp.where(bad == 0, table_ref[half * peers * peers + at], table_ref[0])

    for part, out in enumerate((o0, o1, o2, o3)):
        q = ((me - turns[part] + peers) & (peers - 1)) ^ me

        def move(r, carry, part=part, out=out, q=q):
            slot = all_ref[q, part * quarter + r] & (n - 1)
            list_ref[part * quarter + r] = slot
            out[r] = cent_ref[slot]
            return carry

        lax.fori_loop(0, quarter, move, 0, unroll=8)


def pack_centroids(me, table, everyone, cent, peers):
    n = cent.shape[0]
    quarter = jax.ShapeDtypeStruct((n // 4,) + cent.shape[1:], cent.dtype)
    return pl.pallas_call(
        lambda *refs: pack_kernel(peers, *refs),
        out_shape=(quarter,) * 4 + (jax.ShapeDtypeStruct((n,), I32), jax.ShapeDtypeStruct((2,), I32)),
        in_specs=[SM, SM, SM, VM],
        out_specs=(VM,) * 4 + (SM, SM),
        compiler_params=params(),
        name="pack_centroids",
    )(me, table, everyone, cent)


def place_kernel(list_ref, i0, i1, i2, i3, out_ref):
    n = out_ref.shape[0]
    quarter = n // 4
    for part, src in enumerate((i0, i1, i2, i3)):

        def move(r, carry, part=part, src=src):
            out_ref[list_ref[part * quarter + r] & (n - 1)] = src[r]
            return carry

        lax.fori_loop(0, quarter, move, 0, unroll=8)


def place_centroids(slot_list, parts):
    q = parts[0].shape
    return pl.pallas_call(
        place_kernel,
        out_shape=jax.ShapeDtypeStruct((4 * q[0],) + q[1:], BF16),
        in_specs=[SM, VM, VM, VM, VM],
        out_specs=VM,
        compiler_params=params(),
        name="place_centroids",
    )(slot_list, *parts)


def lanes(shape):
    return lax.broadcasted_iota(I32, shape, len(shape) - 1)


def quad(ref, q, at=0):
    x = ref[pl.ds(at + 4 * q, 4)]
    return x.reshape(x.shape[0] * x.shape[1], x.shape[2])


def put(ref, q, value):
    kids = ref.shape[1]
    ref[pl.ds(4 * q, 4)] = value.reshape(4, kids, value.shape[1])


def strip(at, size):
    return pl.ds(at * size if isinstance(at, int) else pl.multiple_of(at * size, size), size)


def loop(rolled, count, body, carry):
    if rolled:
        return lax.fori_loop(0, count, body, carry, unroll=2)
    for q in range(count):
        carry = body(q, carry)
    return carry


def scores_out(out_ref, q, kids, cur_a, cur_b, emb_a, emb_b, tile):
    half = emb_a.shape[0] // 2
    full = nt(cur_a, emb_a) + nt(cur_b, emb_b)
    low = lanes((kids, half)) < half // 2
    for j in range(2):
        r, c = 2 * j * kids, j * half
        out_ref[strip(2 * q + j, kids), :] = jnp.where(
            low, full[r : r + kids, c : c + half], full[r + kids : r + 2 * kids, c : c + half]
        )
    fa, fb = cur_a.astype(F32), cur_b.astype(F32)
    sq = jnp.sum(fa * fa + fb * fb, axis=1, keepdims=True)
    for p in range(4):
        tile = jnp.where(lanes(tile.shape) == 4 * q + p, sq[p * kids : (p + 1) * kids], tile)
    return tile


def first_kernel(rolled, chunk, core_ref, q0, q1, m0, m1, ea_ref, eb_ref, out_ref, ca_ref, cb_ref):
    count, kids, _ = ca_ref.shape
    wide = 2 * ea_ref.shape[1]
    even = core_ref[0] == 0
    diag = lax.broadcasted_iota(I32, (wide, wide), 0) == lanes((wide, wide))
    base = (count // 2) * kids

    def body(q, tile):
        emb_a, emb_b = quad(ea_ref, q, chunk * count), quad(eb_ref, q, chunk * count)
        cur_a = jnp.where(even, quad(q0, q), quad(q1, q))
        cur_b = jnp.where(even, quad(m0, q), quad(m1, q))
        put(ca_ref, q, cur_a)
        put(cb_ref, q, cur_b)
        for j in range(2):
            a, b = emb_a[j * wide : (j + 1) * wide], emb_b[j * wide : (j + 1) * wide]
            gram = nt(a, a) + nt(b, b)
            norm = jnp.sum(jnp.where(diag, gram, 0.0), axis=0, keepdims=True)
            out_ref[pl.ds(base + kids + 2 * q + j, 1), :] = norm
        return scores_out(out_ref, q, kids, cur_a, cur_b, emb_a, emb_b, tile)

    out_ref[base : base + kids, :] = loop(rolled, count // 4, body, jnp.zeros((kids, wide), F32))


def update(q, kids, part_ref, got_ref, centre, rows_ref, len_ref, at, emb_a, emb_b, cur_a, cur_b):
    half = emb_a.shape[0] // 2
    lane = lanes((kids, half))
    low = lane < half // 2

    def of_parent(p):
        return jnp.sum(jnp.where(lane == p, centre, 0.0), axis=1, keepdims=True)

    pieces = []
    for j in range(2):
        pair = 2 * q + j
        s = part_ref[strip(pair, kids), :] + got_ref[strip(pair, kids), :]
        p = 2 * pair
        scale = jnp.where(low, of_parent(p), of_parent(p + 1))
        raised = jnp.exp(s * scale * rows_ref[pl.ds(pair, 1), :])
        w = raised / jnp.sum(raised, axis=0, keepdims=True)
        end = jnp.where(low, len_ref[0, at + p], len_ref[0, at + p + 1] + half // 2)
        w = jnp.where(lane < end, w, 0.0)
        none = jnp.zeros((kids, half), BF16)
        for piece in (jnp.where(low, w, 0.0).astype(BF16), jnp.where(low, 0.0, w).astype(BF16)):
            pieces.append(jnp.concatenate([piece, none] if j == 0 else [none, piece], axis=1))
    weights = jnp.concatenate(pieces, axis=0)
    total = jnp.sum(weights.astype(F32), axis=1, keepdims=True) + PRIOR
    new = []
    for emb, cur in ((emb_a, cur_a), (emb_b, cur_b)):
        moments = jnp.dot(weights, emb, preferred_element_type=F32)
        new.append(((moments + PRIOR * cur.astype(F32)) / total).astype(BF16))
    return new


def second_kernel(rolled, chunk, core_ref, len_ref, part_ref, got_ref, ca_ref, cb_ref, ea_ref, eb_ref, na_ref, nb_ref, out_ref, rows_ref):
    count, kids, _ = ca_ref.shape
    base = (count // 2) * kids
    centre = lax.rsqrt(part_ref[base : base + kids, :] + got_ref[base : base + kids, :] + EPS)
    norm = part_ref[base + kids : base + kids + count // 2, :] + got_ref[base + kids : base + kids + count // 2, :]
    rows_ref[...] = lax.rsqrt(norm + EPS) * (1.0 / SHARPNESS)
    at = (2 * chunk + core_ref[0]) * count

    def body(q, tile):
        emb_a, emb_b = quad(ea_ref, q, chunk * count), quad(eb_ref, q, chunk * count)
        new_a, new_b = update(
            q, kids, part_ref, got_ref, centre, rows_ref, len_ref, at, emb_a, emb_b, quad(ca_ref, q), quad(cb_ref, q)
        )
        put(na_ref, q, new_a)
        put(nb_ref, q, new_b)
        return scores_out(out_ref, q, kids, new_a, new_b, emb_a, emb_b, tile)

    out_ref[base : base + kids, :] = loop(rolled, count // 4, body, jnp.zeros((kids, out_ref.shape[1]), F32))


def last_kernel(rolled, chunk, core_ref, len_ref, part_ref, got_ref, rows_ref, ca_ref, cb_ref, ea_ref, eb_ref, na_ref, nb_ref):
    count, kids, _ = ca_ref.shape
    base = (count // 2) * kids
    centre = lax.rsqrt(part_ref[base : base + kids, :] + got_ref[base : base + kids, :] + EPS)
    at = (2 * chunk + core_ref[0]) * count

    def body(q, carry):
        new_a, new_b = update(
            q, kids, part_ref, got_ref, centre, rows_ref, len_ref, at,
            quad(ea_ref, q, chunk * count), quad(eb_ref, q, chunk * count), quad(ca_ref, q), quad(cb_ref, q),
        )
        put(na_ref, q, new_a)
        put(nb_ref, q, new_b)
        return carry

    loop(rolled, count // 4, body, 0)


def call(kernel, rolled, chunk, scalars, arrays, outs, name):
    return pl.pallas_call(
        lambda *refs: kernel(rolled, chunk, *refs),
        out_shape=tuple(jax.ShapeDtypeStruct(s, t) for s, t in outs),
        in_specs=[SM] * len(scalars) + [VM] * len(arrays),
        out_specs=(VM,) * len(outs),
        compiler_params=params(),
        cost_estimate=pl.CostEstimate(flops=10**8, bytes_accessed=6 * 10**6, transcendentals=10**5),
        name=name,
    )(*scalars, *arrays)


def first_pass(chunk, scalars, quarters, blocks, rolled=False):
    shape = quarters[0].shape
    count, kids, _ = shape
    rows = (count // 2) * kids + kids + count // 2
    outs = [((rows, 2 * blocks[0].shape[1]), F32), (shape, BF16), (shape, BF16)]
    return call(first_kernel, rolled, chunk, scalars[:1], [*quarters, *blocks], outs, "first_scores")


def second_pass(chunk, scalars, part, got, blocks, cents, rolled=False):
    shape = cents[0].shape
    count, kids, _ = shape
    wide = part.shape[1]
    outs = [(shape, BF16), (shape, BF16), (((count // 2) * kids + kids, wide), F32), ((count // 2, wide), F32)]
    return call(second_kernel, rolled, chunk, scalars, [part, got, *cents, *blocks], outs, "second_scores")


def last_pass(chunk, scalars, part, got, rows, blocks, cents, rolled=False):
    shape = cents[0].shape
    arrays = [part, got, rows, *cents, *blocks]
    return call(last_kernel, rolled, chunk, scalars, arrays, [(shape, BF16), (shape, BF16)], "last_update")


def across(x, step):
    return lax.ppermute(x, "grp", [(g, g ^ step) for g in range(lax.axis_size("grp"))])


def turned(x, turn):
    peers = lax.axis_size("dp")
    if turn % peers == 0:
        return x
    return lax.ppermute(x, "dp", [(d, (d + turn) % peers) for d in range(peers)])


def fetch(turns, packed):
    return [turned(x, -t) for t, x in zip(turns, packed)]


def give(turns, quarters):
    return [turned(x, t) for t, x in zip(turns, quarters)]


def held(me, by_source):
    peers, n = by_source.shape
    cap = 2 * n // peers
    here = by_source // n == me
    first = jnp.argmax(here, axis=1).astype(I32)
    index = jnp.minimum(first[:, None] + jnp.arange(cap, dtype=I32)[None, :], n - 1)
    return jnp.take_along_axis(by_source, index, axis=1) & (n - 1), jnp.any(here, axis=1)


def holders(me, by_source):
    peers, n = by_source.shape
    return (lax.dynamic_index_in_dim(by_source, me, 0, keepdims=False) // n)[:: 2 * n // peers]


def fetch_any(me, by_source, cent):
    slots, _ = held(me, by_source)
    got = lax.all_to_all(jnp.take(cent, slots, axis=0), "dp", split_axis=0, concat_axis=0, tiled=True)
    mine = jnp.take(got, holders(me, by_source), axis=0)
    quarters = mine.reshape((4, cent.shape[0] // 4) + cent.shape[1:])
    return [quarters[i] for i in range(4)]


def give_any(me, by_source, quarters):
    peers, n = by_source.shape
    cap = 2 * n // peers
    shape = quarters[0].shape
    groups = jnp.stack(quarters).reshape((n // cap, cap) + shape[1:])
    mine = holders(me, by_source)
    at = jnp.argmax(mine[None, :] == jnp.arange(peers, dtype=I32)[:, None], axis=1)
    got = lax.all_to_all(jnp.take(groups, at, axis=0), "dp", split_axis=0, concat_axis=0, tiled=True)
    slots, here = held(me, by_source)
    sources = jnp.argsort(jnp.logical_not(here), stable=True)[: n // cap]
    parts = jnp.take(got, sources, axis=0).reshape((4,) + shape)
    return [parts[i] for i in range(4)] + [jnp.take(slots, sources, axis=0).reshape(n)]


def pairs_of_turns(peers):
    sets = list(itertools.combinations(range(peers), 4))
    lists = [sorted({t[:2] for t in sets}), sorted({t[2:] for t in sets})]
    table = [len(lists[0])] * (2 * peers * peers)
    for half, pairs in enumerate(lists):
        for i, (a, b) in enumerate(pairs):
            table[half * peers * peers + a * peers + b] = i
    return lists, table


def on_device(embeddings, lengths, parent_slot, centroids):
    peers = lax.axis_size("dp")
    me = lax.axis_index("dp").astype(I32)
    core = (lax.axis_index("grp") & 1).astype(I32)
    me1, core1 = me.reshape(1), core.reshape(1)
    slots, perm, lens = sort_parents(me1, parent_slot, lengths, peers)
    keep, send = split_blocks(core1, perm, embeddings)
    blocks = [keep, across(send, 1)]
    scalars = [core1, lens]

    def first(chunk, own):
        part, *c = first_pass(chunk, scalars, list(own) + [across(x, 1) for x in own], blocks)
        return c, part, across(part, 2)

    def second(chunk, state):
        c, part, got = state
        na, nb, part, rows = second_pass(chunk, scalars, part, got, blocks, c)
        return [na, nb], part, across(part, 2), rows

    def last(chunk, state):
        c, part, got, rows = state
        own, other = last_pass(chunk, scalars, part, got, rows, blocks, c)
        other = across(other, 1)
        return [jnp.where(core == 0, own, other), jnp.where(core == 0, other, own)]

    if peers != 8:
        by_source = lax.all_gather(slots, "dp", axis=0, tiled=True)
        quarters = fetch_any(me, by_source, centroids)
        states = [second(c, first(c, quarters[2 * c : 2 * c + 2])) for c in range(2)]
        *parts, slot_list = give_any(me, by_source, last(0, states[0]) + last(1, states[1]))
        return place_centroids(slot_list, parts)

    lists, table = pairs_of_turns(peers)
    everyone = slots
    for step in (1, 2, 4):
        pairs = [(d, d ^ step) for d in range(peers)]
        everyone = jnp.concatenate([everyone, lax.ppermute(everyone, "dp", pairs)], axis=0)
    *packed, slot_list, branch = pack_centroids(me1, jnp.array(table, I32), everyone, centroids, peers)

    def in_order(everyone):
        return jnp.take(everyone, jnp.arange(peers, dtype=I32) ^ me, axis=0)

    def fetched(chunk):
        return lax.switch(
            branch[chunk],
            [lambda p, e, c, turns=turns: tuple(fetch(turns, p)) for turns in lists[chunk]]
            + [lambda p, e, c: tuple(fetch_any(me, in_order(e), c)[2 * chunk : 2 * chunk + 2])],
            packed[2 * chunk : 2 * chunk + 2], everyone, centroids,
        )

    a = first(0, fetched(0))
    b = fetched(1)
    a = second(0, a)
    b = first(1, b)
    a = last(0, a)
    b = second(1, b)
    sent = lax.switch(
        branch[0],
        [lambda x, turns=turns: tuple(give(turns, x)) for turns in lists[0]] + [lambda x: tuple(x)],
        a,
    )
    b = last(1, b)
    return lax.switch(
        branch[1],
        [
            lambda s, a, b, e, l, turns=turns: place_centroids(l, [*s, *give(turns, b)])
            for turns in lists[1]
        ]
        + [lambda s, a, b, e, l: place_any(me, in_order(e), [*a, *b])],
        sent, a, b, everyone, slot_list,
    )


def place_any(me, by_source, quarters):
    *parts, slot_list = give_any(me, by_source, quarters)
    return place_centroids(slot_list, parts)


def solution(mesh):
    return jax.shard_map(
        on_device,
        mesh=mesh,
        in_specs=(P("dp", None, "grp"), P("dp"), P("dp"), P("dp", None, "grp")),
        out_specs=P("dp", None, "grp"),
        check_vma=False,
    )
```

```python
import itertools
import jax
import jax.numpy as jnp
from jax import lax
from jax.sharding import PartitionSpec as P
from jax.experimental import pallas as pl
from jax.experimental.pallas import tpu as pltpu

F32, BF16, I32 = jnp.float32, jnp.bfloat16, jnp.int32
SHARPNESS = 0.02
PRIOR = 1.0
EPS = 1e-06
VMEM_BYTES = 16 * 1024 * 1024


def spec(space):
    return pl.BlockSpec(memory_space=space)


VM, SM, ANY = spec(pltpu.VMEM), spec(pltpu.SMEM), spec(pl.ANY)


def params():
    return pltpu.CompilerParams(vmem_limit_bytes=VMEM_BYTES)


def nt(a, b):
    return lax.dot_general(a, b, (((1,), (1,)), ((), ())), preferred_element_type=F32)


def sort_kernel(shift, peers, me_ref, slot_ref, len_ref, slot_out, perm_out, len_out):
    n = slot_ref.shape[1]
    row = lax.broadcasted_iota(I32, (n, n), 0)
    col = lax.broadcasted_iota(I32, (n, n), 1)
    slots = slot_ref[...]
    turn = (lax.shift_right_logical(slots, shift) - me_ref[0] + peers) & (peers - 1)
    key = (turn * n + lax.broadcasted_iota(I32, (1, n), 1)).astype(F32)
    diag = row == col

    def column(x):
        return jnp.sum(jnp.where(diag, jnp.broadcast_to(x, (n, n)), 0.0), axis=1, keepdims=True)

    keys = jnp.broadcast_to(key, (n, n))
    place = jnp.sum(jnp.where(keys < column(key), 1.0, 0.0), axis=1, keepdims=True)
    hit = jnp.broadcast_to(place, (n, n)).astype(I32) == col

    def sort(x_col):
        return jnp.sum(jnp.where(hit, x_col, 0.0), axis=0, keepdims=True).astype(I32)

    slot_out[...] = sort(column(slots.astype(F32)))
    perm_out[...] = sort(row.astype(F32))
    len_out[...] = sort(column(len_ref[...].astype(F32)))


def sort_parents(me, slots, lengths, peers):
    n = slots.shape[0]
    row = jax.ShapeDtypeStruct((1, n), I32)
    return pl.pallas_call(
        lambda *refs: sort_kernel(n.bit_length() - 1, peers, *refs),
        out_shape=(row, row, row),
        in_specs=[SM, VM, VM],
        out_specs=(VM, VM, VM),
        name="sort_parents",
    )(me, slots.reshape(1, n), lengths.reshape(1, n))


def quarter_of(chunk, core):
    return 2 * chunk + core


def split_kernel(core_ref, perm_ref, emb_ref, *outs):
    count = outs[0].shape[0]
    core = core_ref[0]
    for chunk in range(2):
        for flip in range(2):

            def move(r, carry, out=outs[2 * chunk + flip], at=quarter_of(chunk, core ^ flip) * count):
                out[r] = emb_ref[perm_ref[0, at + r]]
                return carry

            lax.fori_loop(0, count, move, 0, unroll=4)


def split_blocks(core, perm, emb):
    quarter = jax.ShapeDtypeStruct((emb.shape[0] // 4,) + emb.shape[1:], emb.dtype)
    return pl.pallas_call(
        split_kernel,
        out_shape=(quarter,) * 4,
        in_specs=[SM, SM, VM],
        out_specs=(VM,) * 4,
        compiler_params=params(),
        cost_estimate=pl.CostEstimate(flops=0, bytes_accessed=10**5, transcendentals=0),
        name="split_blocks",
    )(core, perm, emb)


def norms_kernel(a0, b0, a1, b1, n0, n1):
    wide = 2 * a0.shape[1]
    diag = lax.broadcasted_iota(I32, (wide, wide), 0) == lanes((wide, wide))
    for a_ref, b_ref, out in ((a0, b0, n0), (a1, b1, n1)):
        for pair in range(out.shape[0]):
            total = 0.0
            for ref in (a_ref, b_ref):
                x = ref[2 * pair : 2 * pair + 2].reshape(wide, ref.shape[2]).astype(F32)
                for at in range(0, x.shape[1], 128):
                    total = total + x[:, at : at + 128] * x[:, at : at + 128]
            column = jnp.sum(total, axis=1, keepdims=True)
            out[pair : pair + 1, :] = jnp.sum(jnp.where(diag, column, 0.0), axis=0, keepdims=True)


def row_norms(blocks):
    count, block, _ = blocks[0].shape
    norm = jax.ShapeDtypeStruct((count // 2, 2 * block), F32)
    return pl.pallas_call(
        norms_kernel,
        out_shape=(norm, norm),
        in_specs=[VM] * 4,
        out_specs=(VM, VM),
        compiler_params=params(),
        cost_estimate=pl.CostEstimate(flops=10**5, bytes_accessed=10**5, transcendentals=0),
        name="row_norms",
    )(*blocks)


def pack_kernel(peers, me_ref, table_ref, all_ref, cent_ref, o0, o1, o2, o3, list_ref, branch_ref):
    n = cent_ref.shape[0]
    quarter = n // 4
    shift = n.bit_length() - 1
    me = me_ref[0]

    def turn_of(q, i):
        return (lax.shift_right_logical(all_ref[q, i * quarter], shift) - (me ^ q) + peers) & (peers - 1)

    turns = [turn_of(0, i) for i in range(4)]
    bad = jnp.int32(0)
    for q in range(1, peers):
        for i in range(4):
            bad = bad | (turn_of(q, i) ^ turns[i])
    bits = sum(lax.shift_left(jnp.int32(1), t) for t in turns)
    branch_ref[0] = jnp.where(bad == 0, table_ref[bits], table_ref[0])

    for part, out in enumerate((o0, o1, o2, o3)):
        group = quarter_of(part // 2, part % 2)
        q = ((me - turns[group] + peers) & (peers - 1)) ^ me

        def move(r, carry, part=part, group=group, out=out, q=q):
            slot = all_ref[q, group * quarter + r] & (n - 1)
            list_ref[part * quarter + r] = slot
            out[r] = cent_ref[slot]
            return carry

        lax.fori_loop(0, quarter, move, 0, unroll=8)


def pack_centroids(me, table, everyone, cent, peers):
    n = cent.shape[0]
    quarter = jax.ShapeDtypeStruct((n // 4,) + cent.shape[1:], cent.dtype)
    return pl.pallas_call(
        lambda *refs: pack_kernel(peers, *refs),
        out_shape=(quarter,) * 4 + (jax.ShapeDtypeStruct((n,), I32), jax.ShapeDtypeStruct((1,), I32)),
        in_specs=[SM, SM, SM, VM],
        out_specs=(VM,) * 4 + (SM, SM),
        compiler_params=params(),
        name="pack_centroids",
    )(me, table, everyone, cent)


def place_kernel(list_ref, i0, i1, i2, i3, out_ref):
    n = out_ref.shape[0]
    quarter = n // 4
    for part, src in enumerate((i0, i1, i2, i3)):

        def move(r, carry, part=part, src=src):
            out_ref[list_ref[part * quarter + r] & (n - 1)] = src[r]
            return carry

        lax.fori_loop(0, quarter, move, 0, unroll=8)


def place_centroids(slot_list, parts):
    q = parts[0].shape
    return pl.pallas_call(
        place_kernel,
        out_shape=jax.ShapeDtypeStruct((4 * q[0],) + q[1:], BF16),
        in_specs=[SM, VM, VM, VM, VM],
        out_specs=VM,
        compiler_params=params(),
        name="place_centroids",
    )(slot_list, *parts)


def lanes(shape):
    return lax.broadcasted_iota(I32, shape, len(shape) - 1)


def quad(ref, q, at=0):
    x = ref[pl.ds(at + 4 * q, 4)]
    return x.reshape(x.shape[0] * x.shape[1], x.shape[2])


def put(ref, q, value):
    kids = ref.shape[1]
    ref[pl.ds(4 * q, 4)] = value.reshape(4, kids, value.shape[1])


def strip(at, size):
    return pl.ds(at * size if isinstance(at, int) else pl.multiple_of(at * size, size), size)


def loop(unroll, count, body, carry):
    if unroll:
        return lax.fori_loop(0, count, body, carry, unroll=unroll)
    for q in range(count):
        carry = body(q, carry)
    return carry


def scores_out(out_ref, q, kids, cur, emb, tile):
    half = emb[0].shape[0] // 2
    part = emb[0].shape[1]
    full = nt(cur[:, :part], emb[0]) + nt(cur[:, part:], emb[1])
    low = lanes((kids, half)) < half // 2
    for j in range(2):
        r, c = 2 * j * kids, j * half
        out_ref[strip(2 * q + j, kids), :] = jnp.where(
            low, full[r : r + kids, c : c + half], full[r + kids : r + 2 * kids, c : c + half]
        )
    wide = cur.astype(F32)
    sq = jnp.sum(wide * wide, axis=1, keepdims=True)
    for p in range(4):
        tile = jnp.where(lanes(tile.shape) == 4 * q + p, sq[p * kids : (p + 1) * kids], tile)
    return tile


def first_kernel(unroll, chunk, core_ref, q0, q1, m0, m1, norm_ref, ea_ref, eb_ref, out_ref, cur_ref):
    count, kids, _ = cur_ref.shape
    even = core_ref[0] == 0
    base = (count // 2) * kids

    def body(q, tile):
        cur = jnp.concatenate(
            [jnp.where(even, quad(q0, q), quad(q1, q)), jnp.where(even, quad(m0, q), quad(m1, q))], axis=1
        )
        put(cur_ref, q, cur)
        return scores_out(out_ref, q, kids, cur, (quad(ea_ref, q), quad(eb_ref, q)), tile)

    out_ref[base : base + kids, :] = loop(unroll, count // 4, body, jnp.zeros((kids, out_ref.shape[1]), F32))
    out_ref[base + kids : base + kids + count // 2, :] = norm_ref[...]


def update(q, kids, part_ref, got_ref, centre, rows_ref, len_ref, at, emb, cur):
    half = emb[0].shape[0] // 2
    lane = lanes((kids, half))
    low = lane < half // 2

    def of_parent(p):
        if isinstance(p, int):
            return centre[:, p : p + 1]
        return jnp.sum(jnp.where(lane == p, centre, 0.0), axis=1, keepdims=True)

    pieces = []
    for j in range(2):
        pair = 2 * q + j
        s = part_ref[strip(pair, kids), :] + got_ref[strip(pair, kids), :]
        p = 2 * pair
        scale = jnp.where(low, of_parent(p), of_parent(p + 1))
        raised = jnp.exp(s * scale * rows_ref[pl.ds(pair, 1), :])
        end = jnp.where(low, len_ref[0, at + p], len_ref[0, at + p + 1] + half // 2)
        w = jnp.where(lane < end, raised / jnp.sum(raised, axis=0, keepdims=True), 0.0)
        none = jnp.zeros((kids, half), BF16)
        for piece in (jnp.where(low, w, 0.0).astype(BF16), jnp.where(low, 0.0, w).astype(BF16)):
            pieces.append(jnp.concatenate([piece, none] if j == 0 else [none, piece], axis=1))
    weights = jnp.concatenate(pieces, axis=0)
    total = jnp.sum(weights.astype(F32), axis=1, keepdims=True) + PRIOR
    moments = jnp.concatenate([jnp.dot(weights, e, preferred_element_type=F32) for e in emb], axis=1)
    return ((moments + PRIOR * cur.astype(F32)) * (1.0 / total)).astype(BF16)


def second_kernel(unroll, chunk, core_ref, len_ref, part_ref, got_ref, cur_ref, ea_ref, eb_ref, new_ref, out_ref, rows_ref):
    count, kids, _ = cur_ref.shape
    base = (count // 2) * kids
    centre = lax.rsqrt(part_ref[base : base + kids, :] + got_ref[base : base + kids, :] + EPS)
    norm = part_ref[base + kids : base + kids + count // 2, :] + got_ref[base + kids : base + kids + count // 2, :]
    rows_ref[...] = lax.rsqrt(norm + EPS) * (1.0 / SHARPNESS)
    at = quarter_of(chunk, core_ref[0]) * count

    def body(q, tile):
        emb = (quad(ea_ref, q), quad(eb_ref, q))
        new = update(q, kids, part_ref, got_ref, centre, rows_ref, len_ref, at, emb, quad(cur_ref, q))
        put(new_ref, q, new)
        return scores_out(out_ref, q, kids, new, emb, tile)

    out_ref[base : base + kids, :] = loop(unroll, count // 4, body, jnp.zeros((kids, out_ref.shape[1]), F32))


def last_kernel(unroll, chunk, core_ref, len_ref, part_ref, got_ref, rows_ref, cur_ref, ea_ref, eb_ref, na_ref, nb_ref):
    count, kids, _ = cur_ref.shape
    part = na_ref.shape[2]
    base = (count // 2) * kids
    centre = lax.rsqrt(part_ref[base : base + kids, :] + got_ref[base : base + kids, :] + EPS)
    at = quarter_of(chunk, core_ref[0]) * count

    def body(q, carry):
        new = update(q, kids, part_ref, got_ref, centre, rows_ref, len_ref, at, (quad(ea_ref, q), quad(eb_ref, q)), quad(cur_ref, q))
        put(na_ref, q, new[:, :part])
        put(nb_ref, q, new[:, part:])
        return carry

    loop(unroll, count // 4, body, 0)


def call(kernel, unroll, chunk, scalars, arrays, outs, name):
    return pl.pallas_call(
        lambda *refs: kernel(unroll, chunk, *refs),
        out_shape=tuple(jax.ShapeDtypeStruct(s, t) for s, t in outs),
        in_specs=[SM] * len(scalars) + [VM] * len(arrays),
        out_specs=(VM,) * len(outs),
        compiler_params=params(),
        cost_estimate=pl.CostEstimate(flops=10**8, bytes_accessed=6 * 10**6, transcendentals=10**5),
        name=name,
    )(*scalars, *arrays)


def first_pass(chunk, scalars, quarters, norm, emb, unroll=0):
    count, kids, part = quarters[0].shape
    rows = (count // 2) * kids + kids + count // 2
    outs = [((rows, norm.shape[1]), F32), ((count, kids, 2 * part), BF16)]
    return call(first_kernel, unroll, chunk, scalars[:1], [*quarters, norm, *emb], outs, "first_scores")


def second_pass(chunk, scalars, part, got, cur, emb, unroll=0):
    count, kids, _ = cur.shape
    wide = part.shape[1]
    outs = [(cur.shape, BF16), (((count // 2) * kids + kids, wide), F32), ((count // 2, wide), F32)]
    return call(second_kernel, unroll, chunk, scalars, [part, got, cur, *emb], outs, "second_scores")


def last_pass(chunk, scalars, part, got, rows, cur, emb, unroll=0):
    half = (cur.shape[0], cur.shape[1], cur.shape[2] // 2)
    outs = [(half, BF16), (half, BF16)]
    return call(last_kernel, unroll, chunk, scalars, [part, got, rows, cur, *emb], outs, "last_update")


def across(x, step):
    return lax.ppermute(x, "grp", [(g, g ^ step) for g in range(lax.axis_size("grp"))])


def turned(x, turn):
    peers = lax.axis_size("dp")
    if turn % peers == 0:
        return x
    return lax.ppermute(x, "dp", [(d, (d + turn) % peers) for d in range(peers)])


def fetch(turns, packed):
    return [turned(x, -t) for t, x in zip(turns, packed)]


def give(turns, quarters):
    return [turned(x, t) for t, x in zip(turns, quarters)]


def held(me, by_source):
    peers, n = by_source.shape
    cap = 2 * n // peers
    here = by_source // n == me
    first = jnp.argmax(here, axis=1).astype(I32)
    index = jnp.minimum(first[:, None] + jnp.arange(cap, dtype=I32)[None, :], n - 1)
    return jnp.take_along_axis(by_source, index, axis=1) & (n - 1), jnp.any(here, axis=1)


def holders(me, by_source):
    peers, n = by_source.shape
    return (lax.dynamic_index_in_dim(by_source, me, 0, keepdims=False) // n)[:: 2 * n // peers]


def fetch_any(me, by_source, cent):
    slots, _ = held(me, by_source)
    got = lax.all_to_all(jnp.take(cent, slots, axis=0), "dp", split_axis=0, concat_axis=0, tiled=True)
    mine = jnp.take(got, holders(me, by_source), axis=0)
    quarters = mine.reshape((4, cent.shape[0] // 4) + cent.shape[1:])
    return [quarters[i] for i in range(4)]


def give_any(me, by_source, quarters):
    peers, n = by_source.shape
    cap = 2 * n // peers
    shape = quarters[0].shape
    groups = jnp.stack(quarters).reshape((n // cap, cap) + shape[1:])
    mine = holders(me, by_source)
    at = jnp.argmax(mine[None, :] == jnp.arange(peers, dtype=I32)[:, None], axis=1)
    got = lax.all_to_all(jnp.take(groups, at, axis=0), "dp", split_axis=0, concat_axis=0, tiled=True)
    slots, here = held(me, by_source)
    sources = jnp.argsort(jnp.logical_not(here), stable=True)[: n // cap]
    parts = jnp.take(got, sources, axis=0).reshape((4,) + shape)
    return [parts[i] for i in range(4)] + [jnp.take(slots, sources, axis=0).reshape(n)]


def sets_of_turns(peers):
    sets = [t for t in itertools.combinations(range(peers), 4) if {1, peers - 1} <= set(t)]
    table = [len(sets)] * (1 << peers)
    for i, turns in enumerate(sets):
        table[sum(1 << t for t in turns)] = i
    return sets, table


def tie(x, *after):
    return lax.optimization_barrier((x, *after))[0]


def on_device(embeddings, lengths, parent_slot, centroids):
    peers = lax.axis_size("dp")
    me = lax.axis_index("dp").astype(I32)
    core = (lax.axis_index("grp") & 1).astype(I32)
    me1, core1 = me.reshape(1), core.reshape(1)
    slots, perm, lens = sort_parents(me1, parent_slot, lengths, peers)
    scalars = [core1, lens]
    fast = peers == 8

    keep_a, send_a, keep_b, send_b = split_blocks(core1, perm, embeddings)
    emb = [(keep_a, across(send_a, 1)), (keep_b, across(send_b, 1))]
    norms = row_norms([*emb[0], *emb[1]])

    def first(chunk, own):
        mates = [across(x, 1) for x in own]
        return first_pass(chunk, scalars, [*own, *mates], norms[chunk], emb[chunk])

    def second(chunk, part, got, cur):
        cur, part, rows = second_pass(chunk, scalars, part, got, cur, emb[chunk])
        return part, rows, cur

    def last(chunk, part, got, rows, cur):
        own, other = last_pass(chunk, scalars, part, got, rows, cur, emb[chunk])
        other = across(other, 1)
        return [jnp.where(core == 0, own, other), jnp.where(core == 0, other, own)]

    if not fast:
        by_source = lax.all_gather(slots, "dp", axis=0, tiled=True)
        quarters = fetch_any(me, by_source, centroids)
        done = []
        for c in range(2):
            part, cur = first(c, [quarters[quarter_of(c, k)] for k in range(2)])
            part, rows, cur = second(c, part, across(part, 2), cur)
            done += last(c, part, across(part, 2), rows, cur)
        return place_any(me, by_source, done)

    sets, table = sets_of_turns(peers)
    everyone = slots
    for step in (1, 2, 4):
        if step == 2:
            everyone = tie(everyone, send_a, send_b)
        pairs = [(d, d ^ step) for d in range(peers)]
        everyone = jnp.concatenate([everyone, lax.ppermute(everyone, "dp", pairs)], axis=0)
    everyone = tie(everyone, *norms)
    *packed, slot_list, branch = pack_centroids(me1, jnp.array(table, I32), everyone, centroids, peers)

    def in_order():
        return jnp.take(everyone, jnp.arange(peers, dtype=I32) ^ me, axis=0)

    def switch(body):
        return lax.switch(branch[0], [lambda turns=turns: body(turns) for turns in sets + [None]])

    def fetched(turns):
        return fetch_any(me, in_order(), centroids) if turns is None else fetch(turns, packed)

    own = switch(fetched)
    state = []
    for c in range(2):
        part, cur = first(c, own[2 * c : 2 * c + 2])
        state.append((part, across(part, 2), cur))
    for c in range(2):
        part, rows, cur = second(c, *state[c])
        state[c] = (part, across(part, 2), rows, cur)
    done = last(0, *state[0]) + last(1, *state[1])

    def finish(turns):
        if turns is None:
            return place_any(me, in_order(), done)
        return place_centroids(slot_list, give(turns, done))

    return switch(finish)


def place_any(me, by_source, quarters):
    *parts, slot_list = give_any(me, by_source, quarters)
    return place_centroids(slot_list, parts)


def solution(mesh):
    return jax.shard_map(
        on_device,
        mesh=mesh,
        in_specs=(P("dp", None, "grp"), P("dp"), P("dp"), P("dp", None, "grp")),
        out_specs=P("dp", None, "grp"),
        check_vma=False,
    )
```

```python
import itertools
import jax
import jax.numpy as jnp
from jax import lax
from jax.sharding import PartitionSpec as P
from jax.experimental import pallas as pl
from jax.experimental.pallas import tpu as pltpu

F32, BF16, I32 = jnp.float32, jnp.bfloat16, jnp.int32
SHARPNESS = 0.02
PRIOR = 1.0
EPS = 1e-06
MIB = 1024 * 1024


def spec(space):
    return pl.BlockSpec(memory_space=space)


VM, SM, HBM = spec(pltpu.VMEM), spec(pltpu.SMEM), spec(pltpu.HBM)


def params(mib=6):
    return pltpu.CompilerParams(vmem_limit_bytes=mib * MIB)


def nt(a, b):
    return lax.dot_general(a, b, (((1,), (1,)), ((), ())), preferred_element_type=F32)


def quarter_of(chunk, core):
    return 2 * chunk + core


def sort_kernel(peers, me_ref, slot_ref, slot_out, perm_out):
    n = slot_ref.shape[1]
    shift = n.bit_length() - 1
    row = lax.broadcasted_iota(I32, (n, n), 0)
    col = lax.broadcasted_iota(I32, (n, n), 1)
    slots = slot_ref[...]
    turn = (lax.shift_right_logical(slots, shift) - me_ref[0] + peers) & (peers - 1)
    key = (turn * n + lax.broadcasted_iota(I32, (1, n), 1)).astype(F32)
    diag = row == col

    def column(x):
        return jnp.sum(jnp.where(diag, jnp.broadcast_to(x, (n, n)), 0.0), axis=1, keepdims=True)

    keys = jnp.broadcast_to(key, (n, n))
    place = jnp.sum(jnp.where(keys < column(key), 1.0, 0.0), axis=1, keepdims=True)
    hit = jnp.broadcast_to(place, (n, n)).astype(I32) == col

    def sort(x_col):
        return jnp.sum(jnp.where(hit, x_col, 0.0), axis=0, keepdims=True).astype(I32)

    slot_out[...] = sort(column(slots.astype(F32)))
    perm_out[...] = sort(row.astype(F32))


def sort_parents(me, slots, peers):
    n = slots.shape[0]
    row = jax.ShapeDtypeStruct((1, n), I32)
    return pl.pallas_call(
        lambda *refs: sort_kernel(peers, *refs),
        out_shape=(row, row),
        in_specs=[SM, VM],
        out_specs=(VM, VM),
        name="sort_parents",
    )(me, slots.reshape(1, n))


def split_kernel(core_ref, perm_ref, emb_ref, cent_ref, *outs):
    count = outs[0].shape[0]
    core = core_ref[0]
    for part, out in enumerate(outs[:4]):

        def move(r, carry, out=out, at=quarter_of(part // 2, core ^ (part % 2)) * count):
            out[r] = emb_ref[perm_ref[0, at + r]]
            return carry

        lax.fori_loop(0, count, move, 0, unroll=4)
    outs[4][...] = cent_ref[...]


def split_blocks(core, perm, emb, cent):
    quarter = jax.ShapeDtypeStruct((emb.shape[0] // 4,) + emb.shape[1:], emb.dtype)
    return pl.pallas_call(
        split_kernel,
        out_shape=(quarter,) * 4 + (jax.ShapeDtypeStruct(cent.shape, cent.dtype),),
        in_specs=[SM, SM, VM, VM],
        out_specs=(VM,) * 5,
        compiler_params=params(12),
        cost_estimate=pl.CostEstimate(flops=0, bytes_accessed=10**5, transcendentals=0),
        name="split_blocks",
    )(core, perm, emb, cent)


def norms_kernel(a0, b0, a1, b1, n0, n1):
    wide = 2 * a0.shape[1]
    diag = lax.broadcasted_iota(I32, (wide, wide), 0) == lanes((wide, wide))
    for a_ref, b_ref, out in ((a0, b0, n0), (a1, b1, n1)):
        for pair in range(out.shape[0]):
            total = 0.0
            for ref in (a_ref, b_ref):
                x = ref[2 * pair : 2 * pair + 2].reshape(wide, ref.shape[2]).astype(F32)
                for at in range(0, x.shape[1], 128):
                    total = total + x[:, at : at + 128] * x[:, at : at + 128]
            column = jnp.sum(total, axis=1, keepdims=True)
            out[pair : pair + 1, :] = jnp.sum(jnp.where(diag, column, 0.0), axis=0, keepdims=True)


def row_norms(blocks):
    count, block, _ = blocks[0].shape
    norm = jax.ShapeDtypeStruct((count // 2, 2 * block), F32)
    return pl.pallas_call(
        norms_kernel,
        out_shape=(norm, norm),
        in_specs=[VM] * 4,
        out_specs=(VM, VM),
        compiler_params=params(),
        cost_estimate=pl.CostEstimate(flops=10**5, bytes_accessed=10**5, transcendentals=0),
        name="row_norms",
    )(*blocks)


def pack_kernel(peers, me_ref, table_ref, r0, r1, r2, r3, cent_ref, o0, o1, o2, o3, list_ref, branch_ref):
    n = cent_ref.shape[0]
    quarter = n // 4
    shift = n.bit_length() - 1
    me = me_ref[0]
    rows = (r0, r1, r2, r3)

    def turn_of(q, i):
        slot = rows[q // 2][q % 2, i * quarter]
        return (lax.shift_right_logical(slot, shift) - (me ^ q) + peers) & (peers - 1)

    turns = [turn_of(0, i) for i in range(4)]
    bad = jnp.int32(0)
    for q in range(1, peers):
        for i in range(4):
            bad = bad | (turn_of(q, i) ^ turns[i])
    bits = sum(lax.shift_left(jnp.int32(1), t) for t in turns)
    branch_ref[0] = jnp.where(bad == 0, table_ref[bits], table_ref[0])

    for part, out in enumerate((o0, o1, o2, o3)):
        group = quarter_of(part // 2, part % 2)
        q = ((me - turns[group] + peers) & (peers - 1)) ^ me

        def move(r, carry, part=part, group=group, out=out, q=q):
            found = [ref[q & 1, group * quarter + r] for ref in rows]
            low, high = (jnp.where((q & 2) == 0, found[k], found[k + 1]) for k in (0, 2))
            slot = jnp.where((q & 4) == 0, low, high) & (n - 1)
            list_ref[part * quarter + r] = slot
            out[r] = cent_ref[slot]
            return carry

        lax.fori_loop(0, quarter, move, 0, unroll=8)


def pack_centroids(me, table, rows, cent, peers):
    n = cent.shape[0]
    quarter = jax.ShapeDtypeStruct((n // 4,) + cent.shape[1:], cent.dtype)
    return pl.pallas_call(
        lambda *refs: pack_kernel(peers, *refs),
        out_shape=(quarter,) * 4 + (jax.ShapeDtypeStruct((n,), I32), jax.ShapeDtypeStruct((1,), I32)),
        in_specs=[SM] * 6 + [VM],
        out_specs=(VM,) * 4 + (SM, SM),
        compiler_params=params(),
        name="pack_centroids",
    )(me, table, *rows, cent)


def place_kernel(list_ref, i0, i1, i2, i3, out_ref):
    n = out_ref.shape[0]
    quarter = n // 4
    for part, src in enumerate((i0, i1, i2, i3)):

        def move(r, carry, part=part, src=src):
            out_ref[list_ref[part * quarter + r] & (n - 1)] = src[r]
            return carry

        lax.fori_loop(0, quarter, move, 0, unroll=8)


def place_centroids(slot_list, parts):
    q = parts[0].shape
    return pl.pallas_call(
        place_kernel,
        out_shape=jax.ShapeDtypeStruct((4 * q[0],) + q[1:], BF16),
        in_specs=[SM, VM, VM, VM, VM],
        out_specs=VM,
        compiler_params=params(),
        name="place_centroids",
    )(slot_list, *parts)


def lanes(shape):
    return lax.broadcasted_iota(I32, shape, len(shape) - 1)


def quad(ref, q, at=0):
    x = ref[pl.ds(at + 4 * q, 4)]
    return x.reshape(x.shape[0] * x.shape[1], x.shape[2])


def put(ref, q, value):
    kids = ref.shape[1]
    ref[pl.ds(4 * q, 4)] = value.reshape(4, kids, value.shape[1])


def strip(at, size):
    return pl.ds(at * size if isinstance(at, int) else pl.multiple_of(at * size, size), size)


def loop(unroll, count, body, carry):
    if unroll:
        return lax.fori_loop(0, count, body, carry, unroll=unroll)
    for q in range(count):
        carry = body(q, carry)
    return carry


def scores_out(out_ref, q, kids, cur, emb, tile):
    half = emb[0].shape[0] // 2
    part = emb[0].shape[1]
    full = nt(cur[:, :part], emb[0]) + nt(cur[:, part:], emb[1])
    low = lanes((kids, half)) < half // 2
    for j in range(2):
        r, c = 2 * j * kids, j * half
        out_ref[strip(2 * q + j, kids), :] = jnp.where(
            low, full[r : r + kids, c : c + half], full[r + kids : r + 2 * kids, c : c + half]
        )
    wide = cur.astype(F32)
    sq = jnp.sum(wide * wide, axis=1, keepdims=True)
    for p in range(4):
        tile = jnp.where(lanes(tile.shape) == 4 * q + p, sq[p * kids : (p + 1) * kids], tile)
    return tile


def first_kernel(unroll, chunk, core_ref, q0, q1, m0, m1, norm_ref, ea_ref, eb_ref, out_ref, cur_ref):
    count, kids, _ = cur_ref.shape
    even = core_ref[0] == 0
    base = (count // 2) * kids

    def body(q, tile):
        cur = jnp.concatenate(
            [jnp.where(even, quad(q0, q), quad(q1, q)), jnp.where(even, quad(m0, q), quad(m1, q))], axis=1
        )
        put(cur_ref, q, cur)
        return scores_out(out_ref, q, kids, cur, (quad(ea_ref, q), quad(eb_ref, q)), tile)

    out_ref[base : base + kids, :] = loop(unroll, count // 4, body, jnp.zeros((kids, out_ref.shape[1]), F32))
    out_ref[base + kids : base + kids + count // 2, :] = norm_ref[...]


def update(q, kids, part_ref, got_ref, centre, rows_ref, len_refs, at, emb, cur):
    half = emb[0].shape[0] // 2
    lane = lanes((kids, half))
    low = lane < half // 2

    def of_parent(p):
        if isinstance(p, int):
            return centre[:, p : p + 1]
        return jnp.sum(jnp.where(lane == p, centre, 0.0), axis=1, keepdims=True)

    pieces = []
    for j in range(2):
        pair = 2 * q + j
        s = part_ref[strip(pair, kids), :] + got_ref[strip(pair, kids), :]
        p = 2 * pair
        scale = jnp.where(low, of_parent(p), of_parent(p + 1))
        raised = jnp.exp(s * scale * rows_ref[pl.ds(pair, 1), :])
        perm_ref, len_ref = len_refs
        ends = [len_ref[perm_ref[0, at + p + k]] for k in range(2)]
        end = jnp.where(low, ends[0], ends[1] + half // 2)
        w = jnp.where(lane < end, raised / jnp.sum(raised, axis=0, keepdims=True), 0.0)
        none = jnp.zeros((kids, half), BF16)
        for piece in (jnp.where(low, w, 0.0).astype(BF16), jnp.where(low, 0.0, w).astype(BF16)):
            pieces.append(jnp.concatenate([piece, none] if j == 0 else [none, piece], axis=1))
    weights = jnp.concatenate(pieces, axis=0)
    total = jnp.sum(weights.astype(F32), axis=1, keepdims=True) + PRIOR
    moments = jnp.concatenate([jnp.dot(weights, e, preferred_element_type=F32) for e in emb], axis=1)
    return ((moments + PRIOR * cur.astype(F32)) * (1.0 / total)).astype(BF16)


def second_kernel(unroll, chunk, core_ref, perm_ref, len_ref, part_ref, got_ref, cur_ref, ea_ref, eb_ref, new_ref, out_ref, rows_ref):
    count, kids, _ = cur_ref.shape
    base = (count // 2) * kids
    centre = lax.rsqrt(part_ref[base : base + kids, :] + got_ref[base : base + kids, :] + EPS)
    norm = part_ref[base + kids : base + kids + count // 2, :] + got_ref[base + kids : base + kids + count // 2, :]
    rows_ref[...] = lax.rsqrt(norm + EPS) * (1.0 / SHARPNESS)
    at = quarter_of(chunk, core_ref[0]) * count

    def body(q, tile):
        emb = (quad(ea_ref, q), quad(eb_ref, q))
        new = update(q, kids, part_ref, got_ref, centre, rows_ref, (perm_ref, len_ref), at, emb, quad(cur_ref, q))
        put(new_ref, q, new)
        return scores_out(out_ref, q, kids, new, emb, tile)

    out_ref[base : base + kids, :] = loop(unroll, count // 4, body, jnp.zeros((kids, out_ref.shape[1]), F32))


def last_kernel(unroll, chunk, core_ref, perm_ref, len_ref, part_ref, got_ref, rows_ref, cur_ref, ea_ref, eb_ref, na_ref, nb_ref):
    count, kids, _ = cur_ref.shape
    part = na_ref.shape[2]
    base = (count // 2) * kids
    centre = lax.rsqrt(part_ref[base : base + kids, :] + got_ref[base : base + kids, :] + EPS)
    at = quarter_of(chunk, core_ref[0]) * count

    def body(q, carry):
        new = update(q, kids, part_ref, got_ref, centre, rows_ref, (perm_ref, len_ref), at, (quad(ea_ref, q), quad(eb_ref, q)), quad(cur_ref, q))
        put(na_ref, q, new[:, :part])
        put(nb_ref, q, new[:, part:])
        return carry

    loop(unroll, count // 4, body, 0)


def call(kernel, unroll, chunk, scalars, arrays, outs, name):
    return pl.pallas_call(
        lambda *refs: kernel(unroll, chunk, *refs),
        out_shape=tuple(jax.ShapeDtypeStruct(s, t) for s, t in outs),
        in_specs=[SM] * len(scalars) + [VM] * len(arrays),
        out_specs=(VM,) * len(outs),
        compiler_params=params(),
        cost_estimate=pl.CostEstimate(flops=10**8, bytes_accessed=6 * 10**6, transcendentals=10**5),
        name=name,
    )(*scalars, *arrays)


def first_pass(chunk, scalars, quarters, norm, emb, unroll=0):
    count, kids, part = quarters[0].shape
    rows = (count // 2) * kids + kids + count // 2
    outs = [((rows, norm.shape[1]), F32), ((count, kids, 2 * part), BF16)]
    return call(first_kernel, unroll, chunk, scalars[:1], [*quarters, norm, *emb], outs, "first_scores")


def second_pass(chunk, scalars, part, got, cur, emb, unroll=0):
    count, kids, _ = cur.shape
    wide = part.shape[1]
    outs = [(cur.shape, BF16), (((count // 2) * kids + kids, wide), F32), ((count // 2, wide), F32)]
    return call(second_kernel, unroll, chunk, scalars, [part, got, cur, *emb], outs, "second_scores")


def last_pass(chunk, scalars, part, got, rows, cur, emb, unroll=0):
    half = (cur.shape[0], cur.shape[1], cur.shape[2] // 2)
    outs = [(half, BF16), (half, BF16)]
    return call(last_kernel, unroll, chunk, scalars, [part, got, rows, cur, *emb], outs, "last_update")


def across(x, step):
    return lax.ppermute(x, "grp", [(g, g ^ step) for g in range(lax.axis_size("grp"))])


def turned(x, turn):
    peers = lax.axis_size("dp")
    if turn % peers == 0:
        return x
    return lax.ppermute(x, "dp", [(d, (d + turn) % peers) for d in range(peers)])


def swapped(x, step):
    return lax.ppermute(x, "dp", [(d, d ^ step) for d in range(lax.axis_size("dp"))])


def fetch(turns, packed):
    return [turned(x, -t) for t, x in zip(turns, packed)]


def give(turns, quarters):
    return [turned(x, t) for t, x in zip(turns, quarters)]


def held(me, by_source):
    peers, n = by_source.shape
    cap = 2 * n // peers
    here = by_source // n == me
    first = jnp.argmax(here, axis=1).astype(I32)
    index = jnp.minimum(first[:, None] + jnp.arange(cap, dtype=I32)[None, :], n - 1)
    return jnp.take_along_axis(by_source, index, axis=1) & (n - 1), jnp.any(here, axis=1)


def holders(me, by_source):
    peers, n = by_source.shape
    return (lax.dynamic_index_in_dim(by_source, me, 0, keepdims=False) // n)[:: 2 * n // peers]


def fetch_any(me, by_source, cent):
    slots, _ = held(me, by_source)
    got = lax.all_to_all(jnp.take(cent, slots, axis=0), "dp", split_axis=0, concat_axis=0, tiled=True)
    mine = jnp.take(got, holders(me, by_source), axis=0)
    quarters = mine.reshape((4, cent.shape[0] // 4) + cent.shape[1:])
    return [quarters[i] for i in range(4)]


def give_any(me, by_source, quarters):
    peers, n = by_source.shape
    cap = 2 * n // peers
    shape = quarters[0].shape
    groups = jnp.stack(quarters).reshape((n // cap, cap) + shape[1:])
    mine = holders(me, by_source)
    at = jnp.argmax(mine[None, :] == jnp.arange(peers, dtype=I32)[:, None], axis=1)
    got = lax.all_to_all(jnp.take(groups, at, axis=0), "dp", split_axis=0, concat_axis=0, tiled=True)
    slots, here = held(me, by_source)
    sources = jnp.argsort(jnp.logical_not(here), stable=True)[: n // cap]
    parts = jnp.take(got, sources, axis=0).reshape((4,) + shape)
    return [parts[i] for i in range(4)] + [jnp.take(slots, sources, axis=0).reshape(n)]


def sets_of_turns(peers):
    sets = [t for t in itertools.combinations(range(peers), 4) if {1, peers - 1} <= set(t)]
    table = [len(sets)] * (1 << peers)
    for i, turns in enumerate(sets):
        table[sum(1 << t for t in turns)] = i
    return sets, table


def tie(x, *after):
    return lax.optimization_barrier((x, *after))[0]


def on_device(embeddings, lengths, parent_slot, centroids):
    peers = lax.axis_size("dp")
    me = lax.axis_index("dp").astype(I32)
    core = (lax.axis_index("grp") & 1).astype(I32)
    me1, core1 = me.reshape(1), core.reshape(1)
    fast = peers == 8
    slots, perm = sort_parents(me1, parent_slot, peers)
    scalars = [core1, perm, lengths]
    keep_a, send_a, keep_b, send_b, cents = split_blocks(core1, perm, embeddings, centroids)
    if fast:
        pair = jnp.concatenate([slots, swapped(slots, 1)], axis=0)
        send_a, send_b = tie(send_a, pair), tie(send_b, pair)
        rows = [pair] + [swapped(pair, step) for step in (2, 4, 6)]

    emb = [(keep_a, across(send_a, 1)), (keep_b, across(send_b, 1))]
    norms = row_norms([*emb[0], *emb[1]])

    def first(chunk, own, *after):
        mates = [across(x, 1) for x in own]
        return first_pass(chunk, scalars, [*own, *mates], tie(norms[chunk], *after), emb[chunk])

    def second(chunk, part, got, cur):
        cur, part, rows = second_pass(chunk, scalars, part, got, cur, emb[chunk])
        return part, rows, cur

    def last(chunk, part, got, rows, cur):
        return last_pass(chunk, scalars, part, got, rows, cur, emb[chunk])

    def by_quarter(own, other):
        other = across(other, 1)
        return [jnp.where(core == 0, own, other), jnp.where(core == 0, other, own)]

    if not fast:
        by_source = lax.all_gather(slots, "dp", axis=0, tiled=True)
        quarters = fetch_any(me, by_source, centroids)
        done = []
        for c in range(2):
            part, cur = first(c, [quarters[quarter_of(c, k)] for k in range(2)])
            part, rows, cur = second(c, part, across(part, 2), cur)
            done += by_quarter(*last(c, part, across(part, 2), rows, cur))
        return place_any(me, by_source, done)

    sets, table = sets_of_turns(peers)
    rows[0] = tie(rows[0], *norms)
    *packed, slot_list, branch = pack_centroids(me1, jnp.array(table, I32), rows, cents, peers)

    def in_order():
        return jnp.take(jnp.concatenate(rows), jnp.arange(peers, dtype=I32) ^ me, axis=0)

    def switch(body):
        return lax.switch(branch[0], [lambda turns=turns: body(turns) for turns in sets + [None]])

    def fetched(turns):
        return fetch_any(me, in_order(), centroids) if turns is None else fetch(turns, packed)

    own = switch(fetched)
    part_a, cur_a = first(0, own[:2])
    got_a = across(part_a, 2)
    part_b, cur_b = first(1, own[2:], part_a)
    got_b = across(part_b, 2)
    part_a, rows_a, cur_a = second(0, part_a, got_a, tie(cur_a, part_b))
    got_a = across(part_a, 2)
    part_b, rows_b, cur_b = second(1, part_b, got_b, tie(cur_b, part_a))
    got_b = across(part_b, 2)
    own_a, other_a = last(0, part_a, got_a, rows_a, tie(cur_a, part_b))
    own_b, other_b = last(1, part_b, got_b, rows_b, tie(cur_b, own_a))
    done = by_quarter(own_a, tie(other_a, got_b)) + by_quarter(own_b, other_b)

    def finish(turns):
        if turns is None:
            return place_any(me, in_order(), done)
        return place_centroids(slot_list, give(turns, done))

    return switch(finish)


def place_any(me, by_source, quarters):
    *parts, slot_list = give_any(me, by_source, quarters)
    return place_centroids(slot_list, parts)


def solution(mesh):
    return jax.shard_map(
        on_device,
        mesh=mesh,
        in_specs=(P("dp", None, "grp"), P("dp"), P("dp"), P("dp", None, "grp")),
        out_specs=P("dp", None, "grp"),
        check_vma=False,
    )
```

```python
import itertools
import jax
import jax.numpy as jnp
from jax import lax
from jax.sharding import PartitionSpec as P
from jax.experimental import pallas as pl
from jax.experimental.pallas import tpu as pltpu

F32, BF16, I32 = jnp.float32, jnp.bfloat16, jnp.int32
SHARPNESS = 0.02
PRIOR = 1.0
EPS = 1e-06
MIB = 1024 * 1024


def spec(space):
    return pl.BlockSpec(memory_space=space)


VM, SM, HBM = spec(pltpu.VMEM), spec(pltpu.SMEM), spec(pltpu.HBM)


def params(mib=6):
    return pltpu.CompilerParams(vmem_limit_bytes=mib * MIB)


def nt(a, b):
    return lax.dot_general(a, b, (((1,), (1,)), ((), ())), preferred_element_type=F32)


def quarter_of(chunk, core):
    return 2 * chunk + core


def sort_kernel(peers, me_ref, slot_ref, slot_out, perm_out):
    n = slot_ref.shape[1]
    shift = n.bit_length() - 1
    row = lax.broadcasted_iota(I32, (n, n), 0)
    col = lax.broadcasted_iota(I32, (n, n), 1)
    slots = slot_ref[...]
    turn = (lax.shift_right_logical(slots, shift) - me_ref[0] + peers) & (peers - 1)
    key = (turn * n + lax.broadcasted_iota(I32, (1, n), 1)).astype(F32)
    diag = row == col

    def column(x):
        return jnp.sum(jnp.where(diag, jnp.broadcast_to(x, (n, n)), 0.0), axis=1, keepdims=True)

    keys = jnp.broadcast_to(key, (n, n))
    place = jnp.sum(jnp.where(keys < column(key), 1.0, 0.0), axis=1, keepdims=True)
    hit = jnp.broadcast_to(place, (n, n)).astype(I32) == col

    def sort(x_col):
        return jnp.sum(jnp.where(hit, x_col, 0.0), axis=0, keepdims=True).astype(I32)

    slot_out[...] = sort(column(slots.astype(F32)))
    perm_out[...] = sort(row.astype(F32))


def sort_parents(me, slots, peers):
    n = slots.shape[0]
    row = jax.ShapeDtypeStruct((1, n), I32)
    return pl.pallas_call(
        lambda *refs: sort_kernel(peers, *refs),
        out_shape=(row, row),
        in_specs=[SM, VM],
        out_specs=(VM, VM),
        name="sort_parents",
    )(me, slots.reshape(1, n))


def split_kernel(core_ref, perm_ref, emb_hbm, cent_hbm, *refs):
    *outs, cent_out, sems = refs
    count = outs[0].shape[0]
    core = core_ref[0]
    load = pltpu.make_async_copy(cent_hbm, cent_out, sems.at[4])
    load.start()
    for part, out in enumerate(outs):

        def start(r, carry, out=out, at=quarter_of(part // 2, core ^ (part % 2)) * count, sem=sems.at[part]):
            pltpu.make_async_copy(emb_hbm.at[perm_ref[0, at + r]], out.at[r], sem).start()
            return carry

        lax.fori_loop(0, count, start, 0, unroll=8)
    for part, out in enumerate(outs):
        pltpu.make_async_copy(emb_hbm.at[pl.ds(0, count)], out, sems.at[part]).wait()
    load.wait()


def split_blocks(core, perm, emb, cent):
    quarter = jax.ShapeDtypeStruct((emb.shape[0] // 4,) + emb.shape[1:], emb.dtype)
    emb, cent = (pltpu.with_memory_space_constraint(x, pltpu.HBM) for x in (emb, cent))
    return pl.pallas_call(
        split_kernel,
        out_shape=(quarter,) * 4 + (jax.ShapeDtypeStruct(cent.shape, cent.dtype),),
        in_specs=[SM, SM, HBM, HBM],
        out_specs=(VM,) * 5,
        scratch_shapes=[pltpu.SemaphoreType.DMA((5,))],
        compiler_params=params(12),
        cost_estimate=pl.CostEstimate(flops=0, bytes_accessed=10**5, transcendentals=0),
        name="split_blocks",
    )(core, perm, emb, cent)


def rows_kernel(core_ref, perm_ref, len_ref, a0, b0, a1, b1, n0, n1, l0, l1, even):
    even[...] = jnp.where(core_ref[0] == 0, 1.0, 0.0) * jnp.ones_like(even)
    count, block, _ = a0.shape
    wide = 2 * block
    diag = lax.broadcasted_iota(I32, (wide, wide), 0) == lanes((wide, wide))
    lane = lanes((1, wide))
    for chunk, (a_ref, b_ref, norm, live) in enumerate(((a0, b0, n0, l0), (a1, b1, n1, l1))):
        first = quarter_of(chunk, core_ref[0]) * count
        for pair in range(count // 2):
            total = 0.0
            for ref in (a_ref, b_ref):
                x = ref[2 * pair : 2 * pair + 2].reshape(wide, ref.shape[2]).astype(F32)
                for at in range(0, x.shape[1], 128):
                    total = total + x[:, at : at + 128] * x[:, at : at + 128]
            column = jnp.sum(total, axis=1, keepdims=True)
            norm[pair : pair + 1, :] = jnp.sum(jnp.where(diag, column, 0.0), axis=0, keepdims=True)
            ends = [len_ref[perm_ref[0, first + 2 * pair + k]] for k in range(2)]
            end = jnp.where(lane < block, ends[0], ends[1] + block)
            live[pair : pair + 1, :] = jnp.where(lane < end, 1.0, 0.0)


def row_facts(scalars, blocks):
    count, block, _ = blocks[0].shape
    row = jax.ShapeDtypeStruct((count // 2, 2 * block), F32)
    return pl.pallas_call(
        rows_kernel,
        out_shape=(row,) * 4 + (jax.ShapeDtypeStruct((8, 128), F32),),
        in_specs=[SM] * 3 + [VM] * 4,
        out_specs=(VM,) * 5,
        compiler_params=params(),
        cost_estimate=pl.CostEstimate(flops=10**5, bytes_accessed=10**5, transcendentals=0),
        name="row_facts",
    )(*scalars, *blocks)


def pack_kernel(peers, me_ref, table_ref, r0, r1, r2, r3, cent_ref, o0, o1, o2, o3, list_ref, branch_ref):
    n = cent_ref.shape[0]
    quarter = n // 4
    shift = n.bit_length() - 1
    me = me_ref[0]
    rows = (r0, r1, r2, r3)

    def turn_of(q, i):
        slot = rows[q // 2][q % 2, i * quarter]
        return (lax.shift_right_logical(slot, shift) - (me ^ q) + peers) & (peers - 1)

    turns = [turn_of(0, i) for i in range(4)]
    bad = jnp.int32(0)
    for q in range(1, peers):
        for i in range(4):
            bad = bad | (turn_of(q, i) ^ turns[i])
    bits = sum(lax.shift_left(jnp.int32(1), t) for t in turns)
    branch_ref[0] = jnp.where(bad == 0, table_ref[bits], table_ref[0])

    for part, out in enumerate((o0, o1, o2, o3)):
        group = quarter_of(part // 2, part % 2)
        q = ((me - turns[group] + peers) & (peers - 1)) ^ me

        def move(r, carry, part=part, group=group, out=out, q=q):
            found = [ref[q & 1, group * quarter + r] for ref in rows]
            low, high = (jnp.where((q & 2) == 0, found[k], found[k + 1]) for k in (0, 2))
            slot = jnp.where((q & 4) == 0, low, high) & (n - 1)
            list_ref[part * quarter + r] = slot
            out[r] = cent_ref[slot]
            return carry

        lax.fori_loop(0, quarter, move, 0, unroll=8)


def pack_centroids(me, table, rows, cent, peers):
    n = cent.shape[0]
    quarter = jax.ShapeDtypeStruct((n // 4,) + cent.shape[1:], cent.dtype)
    return pl.pallas_call(
        lambda *refs: pack_kernel(peers, *refs),
        out_shape=(quarter,) * 4 + (jax.ShapeDtypeStruct((n,), I32), jax.ShapeDtypeStruct((1,), I32)),
        in_specs=[SM] * 6 + [VM],
        out_specs=(VM,) * 4 + (SM, SM),
        compiler_params=params(),
        name="pack_centroids",
    )(me, table, *rows, cent)


def place_kernel(list_ref, i0, i1, i2, i3, out_ref):
    n = out_ref.shape[0]
    quarter = n // 4
    for part, src in enumerate((i0, i1, i2, i3)):

        def move(r, carry, part=part, src=src):
            out_ref[list_ref[part * quarter + r] & (n - 1)] = src[r]
            return carry

        lax.fori_loop(0, quarter, move, 0, unroll=8)


def place_centroids(slot_list, parts):
    q = parts[0].shape
    return pl.pallas_call(
        place_kernel,
        out_shape=jax.ShapeDtypeStruct((4 * q[0],) + q[1:], BF16),
        in_specs=[SM, VM, VM, VM, VM],
        out_specs=VM,
        compiler_params=params(),
        name="place_centroids",
    )(slot_list, *parts)


def lanes(shape):
    return lax.broadcasted_iota(I32, shape, len(shape) - 1)


def quad(ref, q, at=0):
    x = ref[pl.ds(at + 4 * q, 4)]
    return x.reshape(x.shape[0] * x.shape[1], x.shape[2])


def put(ref, q, value):
    kids = ref.shape[1]
    ref[pl.ds(4 * q, 4)] = value.reshape(4, kids, value.shape[1])


def strip(at, size):
    return pl.ds(at * size if isinstance(at, int) else pl.multiple_of(at * size, size), size)


def loop(unroll, count, body, carry):
    if unroll:
        return lax.fori_loop(0, count, body, carry, unroll=unroll)
    for q in range(count):
        carry = body(q, carry)
    return carry


def scores_out(out_ref, q, kids, cur, emb, tile):
    half = emb[0].shape[0] // 2
    part = emb[0].shape[1]
    full = nt(cur[:, :part], emb[0]) + nt(cur[:, part:], emb[1])
    low = lanes((kids, half)) < half // 2
    for j in range(2):
        r, c = 2 * j * kids, j * half
        out_ref[strip(2 * q + j, kids), :] = jnp.where(
            low, full[r : r + kids, c : c + half], full[r + kids : r + 2 * kids, c : c + half]
        )
    wide = cur.astype(F32)
    sq = jnp.sum(wide * wide, axis=1, keepdims=True)
    for p in range(4):
        tile = jnp.where(lanes(tile.shape) == 4 * q + p, sq[p * kids : (p + 1) * kids], tile)
    return tile


def first_kernel(unroll, even_ref, q0, q1, m0, m1, norm_ref, ea_ref, eb_ref, out_ref, cur_ref):
    count, kids, _ = cur_ref.shape
    base = (count // 2) * kids
    even = jnp.tile(even_ref[0:1, :], (1, q0.shape[2] // 128)) > 0.0

    def pick(a, b):
        return jnp.where(even, a.astype(F32), b.astype(F32)).astype(BF16)

    def body(q, tile):
        cur = jnp.concatenate([pick(quad(q0, q), quad(q1, q)), pick(quad(m0, q), quad(m1, q))], axis=1)
        put(cur_ref, q, cur)
        return scores_out(out_ref, q, kids, cur, (quad(ea_ref, q), quad(eb_ref, q)), tile)

    out_ref[base : base + kids, :] = loop(unroll, count // 4, body, jnp.zeros((kids, out_ref.shape[1]), F32))
    out_ref[base + kids : base + kids + count // 2, :] = norm_ref[...]


def update(q, kids, part_ref, got_ref, centre, rows_ref, live_ref, emb, cur):
    half = emb[0].shape[0] // 2
    lane = lanes((kids, half))
    low = lane < half // 2

    def of_parent(p):
        if isinstance(p, int):
            return centre[:, p : p + 1]
        return jnp.sum(jnp.where(lane == p, centre, 0.0), axis=1, keepdims=True)

    pieces = []
    for j in range(2):
        pair = 2 * q + j
        s = part_ref[strip(pair, kids), :] + got_ref[strip(pair, kids), :]
        p = 2 * pair
        scale = jnp.where(low, of_parent(p), of_parent(p + 1))
        raised = jnp.exp(s * scale * rows_ref[pl.ds(pair, 1), :])
        live = live_ref[pl.ds(pair, 1), :] > 0.0
        w = jnp.where(live, raised / jnp.sum(raised, axis=0, keepdims=True), 0.0)
        none = jnp.zeros((kids, half), BF16)
        for piece in (jnp.where(low, w, 0.0).astype(BF16), jnp.where(low, 0.0, w).astype(BF16)):
            pieces.append(jnp.concatenate([piece, none] if j == 0 else [none, piece], axis=1))
    weights = jnp.concatenate(pieces, axis=0)
    total = jnp.sum(weights.astype(F32), axis=1, keepdims=True) + PRIOR
    moments = jnp.concatenate([jnp.dot(weights, e, preferred_element_type=F32) for e in emb], axis=1)
    return ((moments + PRIOR * cur.astype(F32)) * (1.0 / total)).astype(BF16)


def second_kernel(unroll, live_ref, part_ref, got_ref, cur_ref, ea_ref, eb_ref, new_ref, out_ref, rows_ref):
    count, kids, _ = cur_ref.shape
    base = (count // 2) * kids
    centre = lax.rsqrt(part_ref[base : base + kids, :] + got_ref[base : base + kids, :] + EPS)
    norm = part_ref[base + kids : base + kids + count // 2, :] + got_ref[base + kids : base + kids + count // 2, :]
    rows_ref[...] = lax.rsqrt(norm + EPS) * (1.0 / SHARPNESS)

    def body(q, tile):
        emb = (quad(ea_ref, q), quad(eb_ref, q))
        new = update(q, kids, part_ref, got_ref, centre, rows_ref, live_ref, emb, quad(cur_ref, q))
        put(new_ref, q, new)
        return scores_out(out_ref, q, kids, new, emb, tile)

    out_ref[base : base + kids, :] = loop(unroll, count // 4, body, jnp.zeros((kids, out_ref.shape[1]), F32))


def last_kernel(unroll, live_ref, part_ref, got_ref, rows_ref, cur_ref, ea_ref, eb_ref, na_ref, nb_ref):
    count, kids, _ = cur_ref.shape
    part = na_ref.shape[2]
    base = (count // 2) * kids
    centre = lax.rsqrt(part_ref[base : base + kids, :] + got_ref[base : base + kids, :] + EPS)

    def body(q, carry):
        new = update(q, kids, part_ref, got_ref, centre, rows_ref, live_ref, (quad(ea_ref, q), quad(eb_ref, q)), quad(cur_ref, q))
        put(na_ref, q, new[:, :part])
        put(nb_ref, q, new[:, part:])
        return carry

    loop(unroll, count // 4, body, 0)


def call(kernel, unroll, scalars, arrays, outs, name):
    return pl.pallas_call(
        lambda *refs: kernel(unroll, *refs),
        out_shape=tuple(outs),
        in_specs=[SM] * len(scalars) + [VM] * len(arrays),
        out_specs=(VM,) * len(outs),
        compiler_params=params(),
        cost_estimate=pl.CostEstimate(flops=10**8, bytes_accessed=6 * 10**6, transcendentals=10**5),
        name=name,
    )(*scalars, *arrays)


def first_pass(even, quarters, norm, emb, unroll=0):
    count, kids, part = quarters[0].shape
    rows = (count // 2) * kids + kids + count // 2
    outs = [pltpu.VMEM((rows, norm.shape[1]), F32), pltpu.VMEM((count, kids, 2 * part), BF16)]
    return call(first_kernel, unroll, [], [even, *quarters, norm, *emb], outs, "first_scores")


def second_pass(live, part, got, cur, emb, unroll=0):
    count, kids, _ = cur.shape
    wide = part.shape[1]
    outs = [
        pltpu.VMEM(cur.shape, BF16), pltpu.VMEM(((count // 2) * kids + kids, wide), F32), pltpu.VMEM((count // 2, wide), F32)
    ]
    return call(second_kernel, unroll, [], [live, part, got, cur, *emb], outs, "second_scores")


def last_pass(live, part, got, rows, cur, emb, unroll=0):
    half = pltpu.VMEM((cur.shape[0], cur.shape[1], cur.shape[2] // 2), BF16)
    return call(last_kernel, unroll, [], [live, part, got, rows, cur, *emb], [half, half], "last_update")


def across(x, step):
    return lax.ppermute(x, "grp", [(g, g ^ step) for g in range(lax.axis_size("grp"))])


def turned(x, turn):
    peers = lax.axis_size("dp")
    if turn % peers == 0:
        return x
    return lax.ppermute(x, "dp", [(d, (d + turn) % peers) for d in range(peers)])


def swapped(x, step):
    return lax.ppermute(x, "dp", [(d, d ^ step) for d in range(lax.axis_size("dp"))])


def fetch(turns, packed):
    return [turned(x, -t) for t, x in zip(turns, packed)]


def give(turns, quarters):
    return [turned(x, t) for t, x in zip(turns, quarters)]


def held(me, by_source):
    peers, n = by_source.shape
    cap = 2 * n // peers
    here = by_source // n == me
    first = jnp.argmax(here, axis=1).astype(I32)
    index = jnp.minimum(first[:, None] + jnp.arange(cap, dtype=I32)[None, :], n - 1)
    return jnp.take_along_axis(by_source, index, axis=1) & (n - 1), jnp.any(here, axis=1)


def holders(me, by_source):
    peers, n = by_source.shape
    return (lax.dynamic_index_in_dim(by_source, me, 0, keepdims=False) // n)[:: 2 * n // peers]


def fetch_any(me, by_source, cent):
    slots, _ = held(me, by_source)
    got = lax.all_to_all(jnp.take(cent, slots, axis=0), "dp", split_axis=0, concat_axis=0, tiled=True)
    mine = jnp.take(got, holders(me, by_source), axis=0)
    quarters = mine.reshape((4, cent.shape[0] // 4) + cent.shape[1:])
    return [quarters[i] for i in range(4)]


def give_any(me, by_source, quarters):
    peers, n = by_source.shape
    cap = 2 * n // peers
    shape = quarters[0].shape
    groups = jnp.stack(quarters).reshape((n // cap, cap) + shape[1:])
    mine = holders(me, by_source)
    at = jnp.argmax(mine[None, :] == jnp.arange(peers, dtype=I32)[:, None], axis=1)
    got = lax.all_to_all(jnp.take(groups, at, axis=0), "dp", split_axis=0, concat_axis=0, tiled=True)
    slots, here = held(me, by_source)
    sources = jnp.argsort(jnp.logical_not(here), stable=True)[: n // cap]
    parts = jnp.take(got, sources, axis=0).reshape((4,) + shape)
    return [parts[i] for i in range(4)] + [jnp.take(slots, sources, axis=0).reshape(n)]


def sets_of_turns(peers):
    sets = [t for t in itertools.combinations(range(peers), 4) if {1, peers - 1} <= set(t)]
    table = [len(sets)] * (1 << peers)
    for i, turns in enumerate(sets):
        table[sum(1 << t for t in turns)] = i
    return sets, table


def tie(x, *after):
    return lax.optimization_barrier((x, *after))[0]


def on_device(embeddings, lengths, parent_slot, centroids):
    peers = lax.axis_size("dp")
    me = lax.axis_index("dp").astype(I32)
    core = (lax.axis_index("grp") & 1).astype(I32)
    me1, core1 = me.reshape(1), core.reshape(1)
    fast = peers == 8
    slots, perm = sort_parents(me1, parent_slot, peers)
    scalars = [core1, perm, lengths]
    keep_a, send_a, keep_b, send_b, cents = split_blocks(core1, perm, embeddings, centroids)
    if fast:
        pair = jnp.concatenate([slots, swapped(slots, 1)], axis=0)
        send_a, send_b = tie(send_a, pair), tie(send_b, pair)
        rows = [pair] + [swapped(pair, step) for step in (2, 4, 6)]

    emb = [(keep_a, across(send_a, 1)), (keep_b, across(send_b, 1))]
    facts = row_facts(scalars, [*emb[0], *emb[1]])
    norms, lives = facts[:2], facts[2:4]

    def first(chunk, own, *after):
        mates = [across(x, 1) for x in own]
        return first_pass(facts[4], [*own, *mates], tie(norms[chunk], *after), emb[chunk])

    def second(chunk, part, got, cur):
        cur, part, rows = second_pass(lives[chunk], part, got, cur, emb[chunk])
        return part, rows, cur

    def last(chunk, part, got, rows, cur):
        return last_pass(lives[chunk], part, got, rows, cur, emb[chunk])

    def by_quarter(own, other):
        other = across(other, 1)
        return [jnp.where(core == 0, own, other), jnp.where(core == 0, other, own)]

    if not fast:
        by_source = lax.all_gather(slots, "dp", axis=0, tiled=True)
        quarters = fetch_any(me, by_source, centroids)
        done = []
        for c in range(2):
            part, cur = first(c, [quarters[quarter_of(c, k)] for k in range(2)])
            part, rows, cur = second(c, part, across(part, 2), cur)
            done += by_quarter(*last(c, part, across(part, 2), rows, cur))
        return place_any(me, by_source, done)

    sets, table = sets_of_turns(peers)
    rows[0] = tie(rows[0], *norms)
    *packed, slot_list, branch = pack_centroids(me1, jnp.array(table, I32), rows, cents, peers)

    def in_order():
        return jnp.take(jnp.concatenate(rows), jnp.arange(peers, dtype=I32) ^ me, axis=0)

    def switch(body):
        return lax.switch(branch[0], [lambda turns=turns: body(turns) for turns in sets + [None]])

    def fetched(turns):
        return fetch_any(me, in_order(), centroids) if turns is None else fetch(turns, packed)

    own = switch(fetched)
    part_a, cur_a = first(0, own[:2])
    got_a = across(part_a, 2)
    part_b, cur_b = first(1, own[2:], part_a)
    got_b = across(part_b, 2)
    part_a, rows_a, cur_a = second(0, part_a, got_a, tie(cur_a, part_b))
    got_a = across(part_a, 2)
    part_b, rows_b, cur_b = second(1, part_b, got_b, tie(cur_b, part_a))
    got_b = across(part_b, 2)
    own_a, other_a = last(0, part_a, got_a, rows_a, tie(cur_a, part_b))
    own_b, other_b = last(1, part_b, got_b, rows_b, tie(cur_b, own_a))
    done = by_quarter(own_a, tie(other_a, got_b)) + by_quarter(own_b, other_b)

    def finish(turns):
        if turns is None:
            return place_any(me, in_order(), done)
        return place_centroids(slot_list, give(turns, done))

    return switch(finish)


def place_any(me, by_source, quarters):
    *parts, slot_list = give_any(me, by_source, quarters)
    return place_centroids(slot_list, parts)


def solution(mesh):
    return jax.shard_map(
        on_device,
        mesh=mesh,
        in_specs=(P("dp", None, "grp"), P("dp"), P("dp"), P("dp", None, "grp")),
        out_specs=P("dp", None, "grp"),
        check_vma=False,
    )
```

```python
import itertools
import jax
import jax.numpy as jnp
from jax import lax
from jax.sharding import PartitionSpec as P
from jax.experimental import pallas as pl
from jax.experimental.pallas import tpu as pltpu

F32, BF16, I32 = jnp.float32, jnp.bfloat16, jnp.int32
SHARPNESS = 0.02
PRIOR = 1.0
EPS = 1e-06
MIB = 1024 * 1024


def spec(space):
    return pl.BlockSpec(memory_space=space)


VM, SM, HBM = spec(pltpu.VMEM), spec(pltpu.SMEM), spec(pltpu.HBM)


def params(mib=6):
    return pltpu.CompilerParams(vmem_limit_bytes=mib * MIB)


def nt(a, b):
    return lax.dot_general(a, b, (((1,), (1,)), ((), ())), preferred_element_type=F32)


def quarter_of(chunk, core):
    return 2 * chunk + core


def sort_kernel(peers, me_ref, slot_ref, slot_out, perm_out):
    n = slot_ref.shape[1]
    shift = n.bit_length() - 1
    row = lax.broadcasted_iota(I32, (n, n), 0)
    col = lax.broadcasted_iota(I32, (n, n), 1)
    slots = slot_ref[...]
    turn = (lax.shift_right_logical(slots, shift) - me_ref[0] + peers) & (peers - 1)
    key = (turn * n + lax.broadcasted_iota(I32, (1, n), 1)).astype(F32)
    diag = row == col

    def column(x):
        return jnp.sum(jnp.where(diag, jnp.broadcast_to(x, (n, n)), 0.0), axis=1, keepdims=True)

    keys = jnp.broadcast_to(key, (n, n))
    place = jnp.sum(jnp.where(keys < column(key), 1.0, 0.0), axis=1, keepdims=True)
    hit = jnp.broadcast_to(place, (n, n)).astype(I32) == col

    def sort(x_col):
        return jnp.sum(jnp.where(hit, x_col, 0.0), axis=0, keepdims=True).astype(I32)

    slot_out[...] = sort(column(slots.astype(F32)))
    perm_out[...] = sort(row.astype(F32))


def sort_parents(me, slots, peers):
    n = slots.shape[0]
    row = jax.ShapeDtypeStruct((1, n), I32)
    return pl.pallas_call(
        lambda *refs: sort_kernel(peers, *refs),
        out_shape=(row, row),
        in_specs=[SM, VM],
        out_specs=(VM, VM),
        name="sort_parents",
    )(me, slots.reshape(1, n))


def split_kernel(core_ref, perm_hbm, emb_hbm, cent_hbm, *refs):
    *outs, cent_out, even, perm_ref, sems = refs
    order = pltpu.make_async_copy(perm_hbm, perm_ref, sems.at[5])
    order.start()
    count = outs[0].shape[0]
    core = core_ref[0]
    load = pltpu.make_async_copy(cent_hbm, cent_out, sems.at[4])
    load.start()
    even[...] = jnp.where(core == 0, 1.0, 0.0) * jnp.ones_like(even)
    order.wait()
    for part, out in enumerate(outs):

        def start(r, carry, out=out, at=quarter_of(part // 2, core ^ (part % 2)) * count, sem=sems.at[part]):
            pltpu.make_async_copy(emb_hbm.at[perm_ref[0, at + r]], out.at[r], sem).start()
            return carry

        lax.fori_loop(0, count, start, 0, unroll=8)
    for part, out in enumerate(outs):
        pltpu.make_async_copy(emb_hbm.at[pl.ds(0, count)], out, sems.at[part]).wait()
    load.wait()


def split_blocks(core, perm, emb, cent):
    quarter = jax.ShapeDtypeStruct((emb.shape[0] // 4,) + emb.shape[1:], emb.dtype)
    perm, emb, cent = (pltpu.with_memory_space_constraint(x, pltpu.HBM) for x in (perm, emb, cent))
    return pl.pallas_call(
        split_kernel,
        out_shape=(quarter,) * 4 + (jax.ShapeDtypeStruct(cent.shape, cent.dtype), jax.ShapeDtypeStruct((8, 128), F32)),
        in_specs=[SM, HBM, HBM, HBM],
        out_specs=(VM,) * 6,
        scratch_shapes=[pltpu.SMEM(perm.shape, I32), pltpu.SemaphoreType.DMA((6,))],
        compiler_params=params(12),
        cost_estimate=pl.CostEstimate(flops=0, bytes_accessed=10**5, transcendentals=0),
        name="split_blocks",
    )(core, perm, emb, cent)


def norms_kernel(a0, b0, a1, b1, n0, n1):
    wide = 2 * a0.shape[1]
    diag = lax.broadcasted_iota(I32, (wide, wide), 0) == lanes((wide, wide))
    for a_ref, b_ref, norm in ((a0, b0, n0), (a1, b1, n1)):
        for pair in range(norm.shape[0]):
            total = 0.0
            for ref in (a_ref, b_ref):
                x = ref[2 * pair : 2 * pair + 2].reshape(wide, ref.shape[2]).astype(F32)
                for at in range(0, x.shape[1], 128):
                    total = total + x[:, at : at + 128] * x[:, at : at + 128]
            column = jnp.sum(total, axis=1, keepdims=True)
            norm[pair : pair + 1, :] = jnp.sum(jnp.where(diag, column, 0.0), axis=0, keepdims=True)


def live_kernel(block, core_ref, perm_ref, len_ref, l0, l1):
    count = 2 * l0.shape[0]
    lane = lanes((1, 2 * block))
    for chunk, live in enumerate((l0, l1)):
        first = quarter_of(chunk, core_ref[0]) * count
        for pair in range(count // 2):
            ends = [len_ref[perm_ref[0, first + 2 * pair + k]] for k in range(2)]
            live[pair : pair + 1, :] = jnp.where(lane < jnp.where(lane < block, ends[0], ends[1] + block), 1.0, 0.0)


def row_facts(kernel, count, block, scalars, arrays, name):
    row = jax.ShapeDtypeStruct((count // 2, 2 * block), F32)
    return pl.pallas_call(
        kernel,
        out_shape=(row, row),
        in_specs=[SM] * len(scalars) + [VM] * len(arrays),
        out_specs=(VM, VM),
        compiler_params=params(),
        cost_estimate=pl.CostEstimate(flops=10**5, bytes_accessed=10**5, transcendentals=0),
        name=name,
    )(*scalars, *arrays)


def pack_kernel(peers, me_ref, table_ref, r0, r1, r2, r3, cent_ref, o0, o1, o2, o3, list_ref, branch_ref):
    n = cent_ref.shape[0]
    quarter = n // 4
    shift = n.bit_length() - 1
    me = me_ref[0]
    rows = (r0, r1, r2, r3)

    def turn_of(q, i):
        slot = rows[q // 2][q % 2, i * quarter]
        return (lax.shift_right_logical(slot, shift) - (me ^ q) + peers) & (peers - 1)

    turns = [turn_of(0, i) for i in range(4)]
    bad = jnp.int32(0)
    for q in range(1, peers):
        for i in range(4):
            bad = bad | (turn_of(q, i) ^ turns[i])
    bits = sum(lax.shift_left(jnp.int32(1), t) for t in turns)
    branch_ref[0] = jnp.where(bad == 0, table_ref[bits], table_ref[0])

    for part, out in enumerate((o0, o1, o2, o3)):
        group = quarter_of(part // 2, part % 2)
        q = ((me - turns[group] + peers) & (peers - 1)) ^ me

        for k, row_ref in enumerate(rows):

            @pl.when(q // 2 == k)
            def _(part=part, group=group, out=out, q=q, row_ref=row_ref):
                def move(r, carry):
                    slot = row_ref[q & 1, group * quarter + r] & (n - 1)
                    list_ref[part * quarter + r] = slot
                    out[r] = cent_ref[slot]
                    return carry

                lax.fori_loop(0, quarter, move, 0, unroll=8)


def pack_centroids(me, table, rows, cent, peers):
    n = cent.shape[0]
    quarter = jax.ShapeDtypeStruct((n // 4,) + cent.shape[1:], cent.dtype)
    return pl.pallas_call(
        lambda *refs: pack_kernel(peers, *refs),
        out_shape=(quarter,) * 4 + (jax.ShapeDtypeStruct((n,), I32), jax.ShapeDtypeStruct((1,), I32)),
        in_specs=[SM] * 6 + [VM],
        out_specs=(VM,) * 4 + (SM, SM),
        compiler_params=params(),
        name="pack_centroids",
    )(me, table, *rows, cent)


def place_kernel(list_ref, i0, i1, i2, i3, out_ref):
    n = out_ref.shape[0]
    quarter = n // 4
    for part, src in enumerate((i0, i1, i2, i3)):

        def move(r, carry, part=part, src=src):
            out_ref[list_ref[part * quarter + r] & (n - 1)] = src[r]
            return carry

        lax.fori_loop(0, quarter, move, 0, unroll=8)


def place_centroids(slot_list, parts):
    q = parts[0].shape
    return pl.pallas_call(
        place_kernel,
        out_shape=jax.ShapeDtypeStruct((4 * q[0],) + q[1:], BF16),
        in_specs=[SM, VM, VM, VM, VM],
        out_specs=VM,
        compiler_params=params(),
        name="place_centroids",
    )(slot_list, *parts)


def lanes(shape):
    return lax.broadcasted_iota(I32, shape, len(shape) - 1)


def quad(ref, q, at=0):
    x = ref[pl.ds(at + 4 * q, 4)]
    return x.reshape(x.shape[0] * x.shape[1], x.shape[2])


def put(ref, q, value):
    kids = ref.shape[1]
    ref[pl.ds(4 * q, 4)] = value.reshape(4, kids, value.shape[1])


def strip(at, size):
    return pl.ds(at * size if isinstance(at, int) else pl.multiple_of(at * size, size), size)


def loop(unroll, count, body, carry):
    if unroll:
        return lax.fori_loop(0, count, body, carry, unroll=unroll)
    for q in range(count):
        carry = body(q, carry)
    return carry


def scores_out(out_ref, q, kids, cur, emb, tile):
    half = emb[0].shape[0] // 2
    part = emb[0].shape[1]
    full = nt(cur[:, :part], emb[0]) + nt(cur[:, part:], emb[1])
    low = lanes((kids, half)) < half // 2
    for j in range(2):
        r, c = 2 * j * kids, j * half
        out_ref[strip(2 * q + j, kids), :] = jnp.where(
            low, full[r : r + kids, c : c + half], full[r + kids : r + 2 * kids, c : c + half]
        )
    wide = cur.astype(F32)
    sq = jnp.sum(wide * wide, axis=1, keepdims=True)
    for p in range(4):
        tile = jnp.where(lanes(tile.shape) == 4 * q + p, sq[p * kids : (p + 1) * kids], tile)
    return tile


def first_kernel(late, *refs):
    even_ref, m0, m1, norm_ref, ea_ref = refs[:5]
    far, (out_ref, cur_ref), held, sems = refs[-2 * late - 3 : -late - 3], refs[-late - 3 : -late - 1], refs[-late - 1 : -1], refs[-1]
    loads = [pltpu.make_async_copy(hbm, ref, sems.at[k]) for k, (hbm, ref) in enumerate(zip(far, held))]
    q0, q1, eb_ref = (*held, refs[5])[:3]
    for load in loads:
        load.start()
    count, kids, part = q0.shape
    base = (count // 2) * kids
    even = jnp.tile(even_ref[0:1, :], (1, part // 128)) > 0.0
    tile = jnp.zeros((kids, out_ref.shape[1]), F32)
    out_ref[base + kids : base + kids + count // 2, :] = norm_ref[...]
    for at, (even_one, odd_one), emb_ref in ((0, (q0, q1), ea_ref), (part, (m0, m1), eb_ref)):
        for load in loads[:2] if at == 0 else loads[2:]:
            load.wait()
        for q in range(count // 4):
            cur = jnp.where(even, quad(even_one, q).astype(F32), quad(odd_one, q).astype(F32))
            sq = jnp.sum(cur * cur, axis=1, keepdims=True)
            for p in range(4):
                here = jnp.where(lanes(tile.shape) == 4 * q + p, sq[p * kids : (p + 1) * kids], 0.0)
                tile = tile + here
            cur = cur.astype(BF16)
            cur_ref[4 * q : 4 * q + 4, :, at : at + part] = cur.reshape(4, kids, part)
            emb = quad(emb_ref, q)
            full = nt(cur, emb)
            half = emb.shape[0] // 2
            low = lanes((kids, half)) < half // 2
            for j in range(2):
                r, c = 2 * j * kids, j * half
                s = jnp.where(low, full[r : r + kids, c : c + half], full[r + kids : r + 2 * kids, c : c + half])
                rows = strip(2 * q + j, kids)
                out_ref[rows, :] = s if at == 0 else out_ref[rows, :] + s
    out_ref[base : base + kids, :] = tile


def update(q, kids, part_ref, got_ref, centre, rows_ref, live_ref, emb, cur):
    half = emb[0].shape[0] // 2
    lane = lanes((kids, half))
    low = lane < half // 2

    def of_parent(p):
        if isinstance(p, int):
            return centre[:, p : p + 1]
        return jnp.sum(jnp.where(lane == p, centre, 0.0), axis=1, keepdims=True)

    pieces = []
    for j in range(2):
        pair = 2 * q + j
        s = part_ref[strip(pair, kids), :] + got_ref[strip(pair, kids), :]
        p = 2 * pair
        scale = jnp.where(low, of_parent(p), of_parent(p + 1))
        raised = jnp.exp(s * scale * rows_ref[pl.ds(pair, 1), :])
        live = live_ref[pl.ds(pair, 1), :] > 0.0
        w = jnp.where(live, raised / jnp.sum(raised, axis=0, keepdims=True), 0.0)
        none = jnp.zeros((kids, half), BF16)
        for piece in (jnp.where(low, w, 0.0).astype(BF16), jnp.where(low, 0.0, w).astype(BF16)):
            pieces.append(jnp.concatenate([piece, none] if j == 0 else [none, piece], axis=1))
    weights = jnp.concatenate(pieces, axis=0)
    total = jnp.sum(weights.astype(F32), axis=1, keepdims=True) + PRIOR
    moments = jnp.concatenate([jnp.dot(weights, e, preferred_element_type=F32) for e in emb], axis=1)
    return ((moments + PRIOR * cur.astype(F32)) * (1.0 / total)).astype(BF16)


def second_kernel(unroll, live_ref, part_ref, got_ref, cur_ref, ea_ref, eb_ref, new_ref, out_ref, rows_ref):
    count, kids, _ = cur_ref.shape
    base = (count // 2) * kids
    centre = lax.rsqrt(part_ref[base : base + kids, :] + got_ref[base : base + kids, :] + EPS)
    norm = part_ref[base + kids : base + kids + count // 2, :] + got_ref[base + kids : base + kids + count // 2, :]
    rows_ref[...] = lax.rsqrt(norm + EPS) * (1.0 / SHARPNESS)

    def body(q, tile):
        emb = (quad(ea_ref, q), quad(eb_ref, q))
        new = update(q, kids, part_ref, got_ref, centre, rows_ref, live_ref, emb, quad(cur_ref, q))
        put(new_ref, q, new)
        return scores_out(out_ref, q, kids, new, emb, tile)

    out_ref[base : base + kids, :] = loop(unroll, count // 4, body, jnp.zeros((kids, out_ref.shape[1]), F32))


def last_kernel(unroll, live_ref, part_ref, got_ref, rows_ref, cur_ref, ea_ref, eb_ref, na_ref, nb_ref):
    count, kids, _ = cur_ref.shape
    part = na_ref.shape[2]
    base = (count // 2) * kids
    centre = lax.rsqrt(part_ref[base : base + kids, :] + got_ref[base : base + kids, :] + EPS)

    def body(q, carry):
        new = update(q, kids, part_ref, got_ref, centre, rows_ref, live_ref, (quad(ea_ref, q), quad(eb_ref, q)), quad(cur_ref, q))
        put(na_ref, q, new[:, :part])
        put(nb_ref, q, new[:, part:])
        return carry

    loop(unroll, count // 4, body, 0)


def call(kernel, unroll, scalars, arrays, outs, name):
    return pl.pallas_call(
        lambda *refs: kernel(unroll, *refs),
        out_shape=tuple(outs),
        in_specs=[SM] * len(scalars) + [VM] * len(arrays),
        out_specs=(VM,) * len(outs),
        compiler_params=params(),
        cost_estimate=pl.CostEstimate(flops=10**8, bytes_accessed=6 * 10**6, transcendentals=10**5),
        name=name,
    )(*scalars, *arrays)


def first_pass(even, own, mates, norm, emb, far):
    count, kids, part = own[0].shape
    rows = (count // 2) * kids + kids + count // 2
    near = [even, *mates, norm, *emb[: 1 if far else 2]]
    late = [pltpu.with_memory_space_constraint(x, pltpu.HBM) for x in (*own, *emb[1 : 2 if far else 1])]
    return pl.pallas_call(
        lambda *refs: first_kernel(len(late), *refs),
        out_shape=(pltpu.VMEM((rows, norm.shape[1]), F32), pltpu.VMEM((count, kids, 2 * part), BF16)),
        in_specs=[VM] * len(near) + [HBM] * len(late),
        out_specs=(VM, VM),
        scratch_shapes=[pltpu.VMEM(x.shape, BF16) for x in late] + [pltpu.SemaphoreType.DMA((len(late),))],
        compiler_params=params(),
        cost_estimate=pl.CostEstimate(flops=10**8, bytes_accessed=6 * 10**6, transcendentals=0),
        name="first_scores",
    )(*near, *late)


def second_pass(live, part, got, cur, emb, unroll=0):
    count, kids, _ = cur.shape
    wide = part.shape[1]
    outs = [
        pltpu.VMEM(cur.shape, BF16), pltpu.VMEM(((count // 2) * kids + kids, wide), F32), pltpu.VMEM((count // 2, wide), F32)
    ]
    return call(second_kernel, unroll, [], [live, part, got, cur, *emb], outs, "second_scores")


def last_pass(live, part, got, rows, cur, emb, unroll=0):
    half = pltpu.VMEM((cur.shape[0], cur.shape[1], cur.shape[2] // 2), BF16)
    return call(last_kernel, unroll, [], [live, part, got, rows, cur, *emb], [half, half], "last_update")


def across(x, step):
    return lax.ppermute(x, "grp", [(g, g ^ step) for g in range(lax.axis_size("grp"))])


def turned(x, turn):
    peers = lax.axis_size("dp")
    if turn % peers == 0:
        return x
    return lax.ppermute(x, "dp", [(d, (d + turn) % peers) for d in range(peers)])


def swapped(x, step):
    return lax.ppermute(x, "dp", [(d, d ^ step) for d in range(lax.axis_size("dp"))])


def fetch(turns, packed):
    return [turned(x, -t) for t, x in zip(turns, packed)]


def give(turns, quarters):
    return [turned(x, t) for t, x in zip(turns, quarters)]


def held(me, by_source):
    peers, n = by_source.shape
    cap = 2 * n // peers
    here = by_source // n == me
    first = jnp.argmax(here, axis=1).astype(I32)
    index = jnp.minimum(first[:, None] + jnp.arange(cap, dtype=I32)[None, :], n - 1)
    return jnp.take_along_axis(by_source, index, axis=1) & (n - 1), jnp.any(here, axis=1)


def holders(me, by_source):
    peers, n = by_source.shape
    return (lax.dynamic_index_in_dim(by_source, me, 0, keepdims=False) // n)[:: 2 * n // peers]


def fetch_any(me, by_source, cent):
    slots, _ = held(me, by_source)
    got = lax.all_to_all(jnp.take(cent, slots, axis=0), "dp", split_axis=0, concat_axis=0, tiled=True)
    mine = jnp.take(got, holders(me, by_source), axis=0)
    quarters = mine.reshape((4, cent.shape[0] // 4) + cent.shape[1:])
    return [quarters[i] for i in range(4)]


def give_any(me, by_source, quarters):
    peers, n = by_source.shape
    cap = 2 * n // peers
    shape = quarters[0].shape
    groups = jnp.stack(quarters).reshape((n // cap, cap) + shape[1:])
    mine = holders(me, by_source)
    at = jnp.argmax(mine[None, :] == jnp.arange(peers, dtype=I32)[:, None], axis=1)
    got = lax.all_to_all(jnp.take(groups, at, axis=0), "dp", split_axis=0, concat_axis=0, tiled=True)
    slots, here = held(me, by_source)
    sources = jnp.argsort(jnp.logical_not(here), stable=True)[: n // cap]
    parts = jnp.take(got, sources, axis=0).reshape((4,) + shape)
    return [parts[i] for i in range(4)] + [jnp.take(slots, sources, axis=0).reshape(n)]


def sets_of_turns(peers):
    sets = [t for t in itertools.combinations(range(peers), 4) if {1, peers - 1} <= set(t)]
    table = [len(sets)] * (1 << peers)
    for i, turns in enumerate(sets):
        table[sum(1 << t for t in turns)] = i
    return sets, table


def tie(x, *after):
    return lax.optimization_barrier((x, *after))[0]


def on_device(embeddings, lengths, parent_slot, centroids):
    peers = lax.axis_size("dp")
    me = lax.axis_index("dp").astype(I32)
    core = (lax.axis_index("grp") & 1).astype(I32)
    me1, core1 = me.reshape(1), core.reshape(1)
    fast = peers == 8
    slots, perm = sort_parents(me1, parent_slot, peers)
    keep_a, send_a, keep_b, send_b, cents, even = split_blocks(core1, perm, embeddings, centroids)
    if fast:
        pair = jnp.concatenate([slots, swapped(slots, 1)], axis=0)
        send_a, send_b = tie(send_a, pair), tie(send_b, pair)
        rows = [pair] + [swapped(pair, step) for step in (2, 4, 6)]

    emb = [(keep_a, across(send_a, 1)), (keep_b, across(send_b, 1))]
    count, block, _ = keep_a.shape
    norms = row_facts(norms_kernel, count, block, [], [*emb[0], *emb[1]], "row_norms")

    def live_rows(*after):
        late = [tie(core1, *after), perm, lengths]
        return row_facts(lambda *refs: live_kernel(block, *refs), count, block, late, [], "live_rows")


    def first(chunk, own, *after):
        mates = [across(x, 1) for x in own]
        return first_pass(even, own, mates, tie(norms[chunk], *after), emb[chunk], chunk == 0)

    def second(chunk, lives, part, got, cur):
        cur, part, rows = second_pass(lives[chunk], part, got, cur, emb[chunk])
        return part, rows, cur

    def last(chunk, lives, part, got, rows, cur):
        return last_pass(lives[chunk], part, got, rows, cur, emb[chunk])

    def by_quarter(own, other):
        other = across(other, 1)
        return [jnp.where(core == 0, own, other), jnp.where(core == 0, other, own)]

    if not fast:
        by_source = lax.all_gather(slots, "dp", axis=0, tiled=True)
        quarters = fetch_any(me, by_source, centroids)
        lives, done = live_rows(), []
        for c in range(2):
            part, cur = first(c, [quarters[quarter_of(c, k)] for k in range(2)])
            part, rows, cur = second(c, lives, part, across(part, 2), cur)
            done += by_quarter(*last(c, lives, part, across(part, 2), rows, cur))
        return place_any(me, by_source, done)

    sets, table = sets_of_turns(peers)
    rows[0] = tie(rows[0], *norms)
    *packed, slot_list, branch = pack_centroids(me1, jnp.array(table, I32), rows, cents, peers)

    def in_order():
        return jnp.take(jnp.concatenate(rows), jnp.arange(peers, dtype=I32) ^ me, axis=0)

    def switch(body):
        return lax.switch(branch[0], [lambda turns=turns: body(turns) for turns in sets + [None]])

    def fetched(turns):
        return fetch_any(me, in_order(), centroids) if turns is None else fetch(turns, packed)

    own = switch(fetched)
    part_a, cur_a = first(0, own[:2])
    got_a = across(part_a, 2)
    part_b, cur_b = first(1, own[2:], part_a)
    got_b = across(part_b, 2)
    lives = live_rows(part_b)
    part_a, rows_a, cur_a = second(0, lives, part_a, got_a, tie(cur_a, part_b))
    got_a = across(part_a, 2)
    part_b, rows_b, cur_b = second(1, lives, part_b, got_b, tie(cur_b, part_a))
    got_b = across(part_b, 2)
    own_a, other_a = last(0, lives, part_a, got_a, rows_a, tie(cur_a, part_b))
    own_b, other_b = last(1, lives, part_b, got_b, rows_b, tie(cur_b, own_a))
    done = by_quarter(own_a, tie(other_a, got_b)) + by_quarter(own_b, other_b)

    def finish(turns):
        if turns is None:
            return place_any(me, in_order(), done)
        return place_centroids(slot_list, give(turns, done))

    return switch(finish)


def place_any(me, by_source, quarters):
    *parts, slot_list = give_any(me, by_source, quarters)
    return place_centroids(slot_list, parts)


def solution(mesh):
    return jax.shard_map(
        on_device,
        mesh=mesh,
        in_specs=(P("dp", None, "grp"), P("dp"), P("dp"), P("dp", None, "grp")),
        out_specs=P("dp", None, "grp"),
        check_vma=False,
    )
```

```python
import itertools
import jax
import jax.numpy as jnp
from jax import lax
from jax.sharding import PartitionSpec as P
from jax.experimental import pallas as pl
from jax.experimental.pallas import tpu as pltpu

F32, BF16, I32 = jnp.float32, jnp.bfloat16, jnp.int32
SHARPNESS = 0.02
PRIOR = 1.0
EPS = 1e-06
MIB = 1024 * 1024


def spec(space):
    return pl.BlockSpec(memory_space=space)


VM, SM, HBM = spec(pltpu.VMEM), spec(pltpu.SMEM), spec(pltpu.HBM)


def params(mib=6):
    return pltpu.CompilerParams(vmem_limit_bytes=mib * MIB)


def nt(a, b):
    return lax.dot_general(a, b, (((1,), (1,)), ((), ())), preferred_element_type=F32)


def quarter_of(chunk, core):
    return 2 * chunk + core


def sort_kernel(peers, me_ref, slot_ref, slot_out, perm_out):
    n = slot_ref.shape[1]
    shift = n.bit_length() - 1
    row = lax.broadcasted_iota(I32, (n, n), 0)
    col = lax.broadcasted_iota(I32, (n, n), 1)
    slots = slot_ref[...]
    turn = (lax.shift_right_logical(slots, shift) - me_ref[0] + peers) & (peers - 1)
    key = (turn * n + lax.broadcasted_iota(I32, (1, n), 1)).astype(F32)
    diag = row == col

    def column(x):
        return jnp.sum(jnp.where(diag, jnp.broadcast_to(x, (n, n)), 0.0), axis=1, keepdims=True)

    keys = jnp.broadcast_to(key, (n, n))
    place = jnp.sum(jnp.where(keys < column(key), 1.0, 0.0), axis=1, keepdims=True)
    hit = jnp.broadcast_to(place, (n, n)).astype(I32) == col

    def sort(x_col):
        return jnp.sum(jnp.where(hit, x_col, 0.0), axis=0, keepdims=True).astype(I32)

    slot_out[...] = sort(column(slots.astype(F32)))
    perm_out[...] = sort(row.astype(F32))


def sort_parents(me, slots, peers):
    n = slots.shape[0]
    row = jax.ShapeDtypeStruct((1, n), I32)
    return pl.pallas_call(
        lambda *refs: sort_kernel(peers, *refs),
        out_shape=(row, row),
        in_specs=[SM, VM],
        out_specs=(VM, VM),
        name="sort_parents",
    )(me, slots.reshape(1, n))


def split_kernel(core_ref, perm_hbm, emb_hbm, cent_hbm, *refs):
    *outs, cent_out, even, perm_ref, sems = refs
    order = pltpu.make_async_copy(perm_hbm, perm_ref, sems.at[5])
    order.start()
    count = outs[0].shape[0]
    core = core_ref[0]
    load = pltpu.make_async_copy(cent_hbm, cent_out, sems.at[4])
    load.start()
    even[...] = jnp.where(core == 0, 1.0, 0.0) * jnp.ones_like(even)
    order.wait()
    for part, out in enumerate(outs):

        def start(r, carry, out=out, at=quarter_of(part // 2, core ^ (part % 2)) * count, sem=sems.at[part]):
            pltpu.make_async_copy(emb_hbm.at[perm_ref[0, at + r]], out.at[r], sem).start()
            return carry

        lax.fori_loop(0, count, start, 0, unroll=8)
    for part, out in enumerate(outs):
        pltpu.make_async_copy(emb_hbm.at[pl.ds(0, count)], out, sems.at[part]).wait()
    load.wait()


def split_blocks(core, perm, emb, cent):
    quarter = jax.ShapeDtypeStruct((emb.shape[0] // 4,) + emb.shape[1:], emb.dtype)
    perm, emb, cent = (pltpu.with_memory_space_constraint(x, pltpu.HBM) for x in (perm, emb, cent))
    return pl.pallas_call(
        split_kernel,
        out_shape=(quarter,) * 4 + (jax.ShapeDtypeStruct(cent.shape, cent.dtype), jax.ShapeDtypeStruct((8, 128), F32)),
        in_specs=[SM, HBM, HBM, HBM],
        out_specs=(VM,) * 6,
        scratch_shapes=[pltpu.SMEM(perm.shape, I32), pltpu.SemaphoreType.DMA((6,))],
        compiler_params=params(12),
        cost_estimate=pl.CostEstimate(flops=0, bytes_accessed=10**5, transcendentals=0),
        name="split_blocks",
    )(core, perm, emb, cent)


def norms_kernel(a0, b0, a1, b1, n0, n1):
    wide = 2 * a0.shape[1]
    diag = lax.broadcasted_iota(I32, (wide, wide), 0) == lanes((wide, wide))
    for a_ref, b_ref, norm in ((a0, b0, n0), (a1, b1, n1)):
        for pair in range(norm.shape[0]):
            total = 0.0
            for ref in (a_ref, b_ref):
                x = ref[2 * pair : 2 * pair + 2].reshape(wide, ref.shape[2]).astype(F32)
                for at in range(0, x.shape[1], 128):
                    total = total + x[:, at : at + 128] * x[:, at : at + 128]
            column = jnp.sum(total, axis=1, keepdims=True)
            norm[pair : pair + 1, :] = jnp.sum(jnp.where(diag, column, 0.0), axis=0, keepdims=True)


def live_kernel(block, core_ref, perm_ref, len_ref, l0, l1):
    count = 2 * l0.shape[0]
    lane = lanes((1, 2 * block))
    for chunk, live in enumerate((l0, l1)):
        first = quarter_of(chunk, core_ref[0]) * count
        for pair in range(count // 2):
            ends = [len_ref[perm_ref[0, first + 2 * pair + k]] for k in range(2)]
            live[pair : pair + 1, :] = jnp.where(lane < jnp.where(lane < block, ends[0], ends[1] + block), 1.0, 0.0)


def row_facts(kernel, count, block, scalars, arrays, name):
    row = jax.ShapeDtypeStruct((count // 2, 2 * block), F32)
    return pl.pallas_call(
        kernel,
        out_shape=(row, row),
        in_specs=[SM] * len(scalars) + [VM] * len(arrays),
        out_specs=(VM, VM),
        compiler_params=params(),
        cost_estimate=pl.CostEstimate(flops=10**5, bytes_accessed=10**5, transcendentals=0),
        name=name,
    )(*scalars, *arrays)


def pack_kernel(peers, me_ref, table_ref, r0, r1, r2, r3, cent_ref, o0, o1, o2, o3, list_ref, branch_ref):
    n = cent_ref.shape[0]
    quarter = n // 4
    shift = n.bit_length() - 1
    me = me_ref[0]
    rows = (r0, r1, r2, r3)

    def turn_of(q, i):
        slot = rows[q // 2][q % 2, i * quarter]
        return (lax.shift_right_logical(slot, shift) - (me ^ q) + peers) & (peers - 1)

    turns = [turn_of(0, i) for i in range(4)]
    bad = jnp.int32(0)
    for q in range(1, peers):
        for i in range(4):
            bad = bad | (turn_of(q, i) ^ turns[i])
    bits = jnp.int32(0)
    for t in turns:
        bits = bits | lax.shift_left(jnp.int32(1), t)
    branch_ref[0] = jnp.where(bad == 0, table_ref[bits], table_ref[0])

    for part, out in enumerate((o0, o1, o2, o3)):
        group = quarter_of(part // 2, part % 2)
        q = ((me - turns[group] + peers) & (peers - 1)) ^ me

        for k, row_ref in enumerate(rows):

            @pl.when(q // 2 == k)
            def _(part=part, group=group, out=out, q=q, row_ref=row_ref):
                def move(r, carry):
                    slot = row_ref[q & 1, group * quarter + r] & (n - 1)
                    list_ref[part * quarter + r] = slot
                    out[r] = cent_ref[slot]
                    return carry

                lax.fori_loop(0, quarter, move, 0, unroll=8)


def pack_centroids(me, table, rows, cent, peers):
    n = cent.shape[0]
    quarter = jax.ShapeDtypeStruct((n // 4,) + cent.shape[1:], cent.dtype)
    return pl.pallas_call(
        lambda *refs: pack_kernel(peers, *refs),
        out_shape=(quarter,) * 4 + (jax.ShapeDtypeStruct((n,), I32), jax.ShapeDtypeStruct((1,), I32)),
        in_specs=[SM] * 6 + [VM],
        out_specs=(VM,) * 4 + (SM, SM),
        compiler_params=params(),
        name="pack_centroids",
    )(me, table, *rows, cent)


def place_kernel(list_ref, i0, i1, i2, i3, out_ref):
    n = out_ref.shape[0]
    quarter = n // 4
    for part, src in enumerate((i0, i1, i2, i3)):

        def move(r, carry, part=part, src=src):
            out_ref[list_ref[part * quarter + r] & (n - 1)] = src[r]
            return carry

        lax.fori_loop(0, quarter, move, 0, unroll=8)


def place_centroids(slot_list, parts):
    q = parts[0].shape
    return pl.pallas_call(
        place_kernel,
        out_shape=jax.ShapeDtypeStruct((4 * q[0],) + q[1:], BF16),
        in_specs=[SM, VM, VM, VM, VM],
        out_specs=VM,
        compiler_params=params(),
        name="place_centroids",
    )(slot_list, *parts)


def lanes(shape):
    return lax.broadcasted_iota(I32, shape, len(shape) - 1)


def quad(ref, q, at=0):
    x = ref[pl.ds(at + 4 * q, 4)]
    return x.reshape(x.shape[0] * x.shape[1], x.shape[2])


def put(ref, q, value):
    kids = ref.shape[1]
    ref[pl.ds(4 * q, 4)] = value.reshape(4, kids, value.shape[1])


def strip(at, size):
    return pl.ds(at * size if isinstance(at, int) else pl.multiple_of(at * size, size), size)


def loop(unroll, count, body, carry):
    if unroll:
        return lax.fori_loop(0, count, body, carry, unroll=unroll)
    for q in range(count):
        carry = body(q, carry)
    return carry


def scores_out(out_ref, q, kids, cur, emb, tile):
    half = emb[0].shape[0] // 2
    part = emb[0].shape[1]
    full = nt(cur[:, :part], emb[0]) + nt(cur[:, part:], emb[1])
    low = lanes((kids, half)) < half // 2
    for j in range(2):
        r, c = 2 * j * kids, j * half
        out_ref[strip(2 * q + j, kids), :] = jnp.where(
            low, full[r : r + kids, c : c + half], full[r + kids : r + 2 * kids, c : c + half]
        )
    wide = cur.astype(F32)
    sq = jnp.sum(wide * wide, axis=1, keepdims=True)
    for p in range(4):
        tile = jnp.where(lanes(tile.shape) == 4 * q + p, sq[p * kids : (p + 1) * kids], tile)
    return tile


def first_kernel(late, *refs):
    even_ref, m0, m1, norm_ref, ea_ref = refs[:5]
    far, (out_ref, cur_ref), held, sems = refs[-2 * late - 3 : -late - 3], refs[-late - 3 : -late - 1], refs[-late - 1 : -1], refs[-1]
    loads = [pltpu.make_async_copy(hbm, ref, sems.at[k]) for k, (hbm, ref) in enumerate(zip(far, held))]
    q0, q1, eb_ref = (*held, refs[5])[:3]
    for load in loads:
        load.start()
    count, kids, part = q0.shape
    base = (count // 2) * kids
    even = jnp.tile(even_ref[0:1, :], (1, part // 128)) > 0.0
    tile = jnp.zeros((kids, out_ref.shape[1]), F32)
    out_ref[base + kids : base + kids + count // 2, :] = norm_ref[...]
    halves = [(0, (q0, q1), ea_ref, loads[:2]), (part, (m0, m1), eb_ref, loads[2:])]
    for step, (at, (even_one, odd_one), emb_ref, needs) in enumerate(halves if late == 3 else halves[::-1]):
        for load in needs:
            load.wait()
        for q in range(count // 4):
            cur = jnp.where(even, quad(even_one, q).astype(F32), quad(odd_one, q).astype(F32))
            sq = jnp.sum(cur * cur, axis=1, keepdims=True)
            for p in range(4):
                here = jnp.where(lanes(tile.shape) == 4 * q + p, sq[p * kids : (p + 1) * kids], 0.0)
                tile = tile + here
            cur = cur.astype(BF16)
            cur_ref[4 * q : 4 * q + 4, :, at : at + part] = cur.reshape(4, kids, part)
            emb = quad(emb_ref, q)
            full = nt(cur, emb)
            half = emb.shape[0] // 2
            low = lanes((kids, half)) < half // 2
            for j in range(2):
                r, c = 2 * j * kids, j * half
                s = jnp.where(low, full[r : r + kids, c : c + half], full[r + kids : r + 2 * kids, c : c + half])
                rows = strip(2 * q + j, kids)
                out_ref[rows, :] = s if step == 0 else out_ref[rows, :] + s
    out_ref[base : base + kids, :] = tile


def update(q, kids, part_ref, got_ref, centre, rows_ref, live_ref, emb, cur):
    half = emb[0].shape[0] // 2
    lane = lanes((kids, half))
    low = lane < half // 2

    def of_parent(p):
        if isinstance(p, int):
            return centre[:, p : p + 1]
        return jnp.sum(jnp.where(lane == p, centre, 0.0), axis=1, keepdims=True)

    pieces = []
    for j in range(2):
        pair = 2 * q + j
        s = part_ref[strip(pair, kids), :] + got_ref[strip(pair, kids), :]
        p = 2 * pair
        scale = jnp.where(low, of_parent(p), of_parent(p + 1))
        raised = jnp.exp(s * scale * rows_ref[pl.ds(pair, 1), :])
        live = live_ref[pl.ds(pair, 1), :] > 0.0
        w = jnp.where(live, raised / jnp.sum(raised, axis=0, keepdims=True), 0.0)
        none = jnp.zeros((kids, half), BF16)
        for piece in (jnp.where(low, w, 0.0).astype(BF16), jnp.where(low, 0.0, w).astype(BF16)):
            pieces.append(jnp.concatenate([piece, none] if j == 0 else [none, piece], axis=1))
    weights = jnp.concatenate(pieces, axis=0)
    total = jnp.sum(weights.astype(F32), axis=1, keepdims=True) + PRIOR
    moments = jnp.concatenate([jnp.dot(weights, e, preferred_element_type=F32) for e in emb], axis=1)
    return ((moments + PRIOR * cur.astype(F32)) * (1.0 / total)).astype(BF16)


def second_kernel(unroll, live_ref, part_ref, got_ref, cur_ref, ea_ref, eb_ref, new_ref, out_ref, rows_ref):
    count, kids, _ = cur_ref.shape
    base = (count // 2) * kids
    centre = lax.rsqrt(part_ref[base : base + kids, :] + got_ref[base : base + kids, :] + EPS)
    norm = part_ref[base + kids : base + kids + count // 2, :] + got_ref[base + kids : base + kids + count // 2, :]
    rows_ref[...] = lax.rsqrt(norm + EPS) * (1.0 / SHARPNESS)

    def body(q, tile):
        emb = (quad(ea_ref, q), quad(eb_ref, q))
        new = update(q, kids, part_ref, got_ref, centre, rows_ref, live_ref, emb, quad(cur_ref, q))
        put(new_ref, q, new)
        return scores_out(out_ref, q, kids, new, emb, tile)

    out_ref[base : base + kids, :] = loop(unroll, count // 4, body, jnp.zeros((kids, out_ref.shape[1]), F32))


def last_kernel(unroll, live_ref, part_ref, got_ref, rows_ref, cur_ref, ea_ref, eb_ref, na_ref, nb_ref):
    count, kids, _ = cur_ref.shape
    part = na_ref.shape[2]
    base = (count // 2) * kids
    centre = lax.rsqrt(part_ref[base : base + kids, :] + got_ref[base : base + kids, :] + EPS)

    def body(q, carry):
        new = update(q, kids, part_ref, got_ref, centre, rows_ref, live_ref, (quad(ea_ref, q), quad(eb_ref, q)), quad(cur_ref, q))
        put(na_ref, q, new[:, :part])
        put(nb_ref, q, new[:, part:])
        return carry

    loop(unroll, count // 4, body, 0)


def call(kernel, unroll, scalars, arrays, outs, name):
    return pl.pallas_call(
        lambda *refs: kernel(unroll, *refs),
        out_shape=tuple(outs),
        in_specs=[SM] * len(scalars) + [VM] * len(arrays),
        out_specs=(VM,) * len(outs),
        compiler_params=params(),
        cost_estimate=pl.CostEstimate(flops=10**8, bytes_accessed=6 * 10**6, transcendentals=10**5),
        name=name,
    )(*scalars, *arrays)


def first_pass(even, own, mates, norm, emb, far):
    count, kids, part = own[0].shape
    rows = (count // 2) * kids + kids + count // 2
    near = [even, *mates, norm, *emb[: 1 if far else 2]]
    late = [pltpu.with_memory_space_constraint(x, pltpu.HBM) for x in (*own, *emb[1 : 2 if far else 1])]
    return pl.pallas_call(
        lambda *refs: first_kernel(len(late), *refs),
        out_shape=(pltpu.VMEM((rows, norm.shape[1]), F32), pltpu.VMEM((count, kids, 2 * part), BF16)),
        in_specs=[VM] * len(near) + [HBM] * len(late),
        out_specs=(VM, VM),
        scratch_shapes=[pltpu.VMEM(x.shape, BF16) for x in late] + [pltpu.SemaphoreType.DMA((len(late),))],
        compiler_params=params(),
        cost_estimate=pl.CostEstimate(flops=10**8, bytes_accessed=6 * 10**6, transcendentals=0),
        name="first_scores",
    )(*near, *late)


def second_pass(live, part, got, cur, emb, unroll=0):
    count, kids, _ = cur.shape
    wide = part.shape[1]
    outs = [
        pltpu.VMEM(cur.shape, BF16), pltpu.VMEM(((count // 2) * kids + kids, wide), F32), pltpu.VMEM((count // 2, wide), F32)
    ]
    return call(second_kernel, unroll, [], [live, part, got, cur, *emb], outs, "second_scores")


def last_pass(live, part, got, rows, cur, emb, unroll=0):
    half = pltpu.VMEM((cur.shape[0], cur.shape[1], cur.shape[2] // 2), BF16)
    return call(last_kernel, unroll, [], [live, part, got, rows, cur, *emb], [half, half], "last_update")


def across(x, step):
    return lax.ppermute(x, "grp", [(g, g ^ step) for g in range(lax.axis_size("grp"))])


def turned(x, turn):
    peers = lax.axis_size("dp")
    if turn % peers == 0:
        return x
    return lax.ppermute(x, "dp", [(d, (d + turn) % peers) for d in range(peers)])


def swapped(x, step):
    return lax.ppermute(x, "dp", [(d, d ^ step) for d in range(lax.axis_size("dp"))])


def fetch(turns, packed):
    return [turned(x, -t) for t, x in zip(turns, packed)]


def give(turns, quarters):
    return [turned(x, t) for t, x in zip(turns, quarters)]


def held(me, by_source):
    peers, n = by_source.shape
    cap = 2 * n // peers
    here = by_source // n == me
    first = jnp.argmax(here, axis=1).astype(I32)
    index = jnp.minimum(first[:, None] + jnp.arange(cap, dtype=I32)[None, :], n - 1)
    return jnp.take_along_axis(by_source, index, axis=1) & (n - 1), jnp.any(here, axis=1)


def holders(me, by_source):
    peers, n = by_source.shape
    return (lax.dynamic_index_in_dim(by_source, me, 0, keepdims=False) // n)[:: 2 * n // peers]


def fetch_any(me, by_source, cent):
    slots, _ = held(me, by_source)
    got = lax.all_to_all(jnp.take(cent, slots, axis=0), "dp", split_axis=0, concat_axis=0, tiled=True)
    mine = jnp.take(got, holders(me, by_source), axis=0)
    quarters = mine.reshape((4, cent.shape[0] // 4) + cent.shape[1:])
    return [quarters[i] for i in range(4)]


def give_any(me, by_source, quarters):
    peers, n = by_source.shape
    cap = 2 * n // peers
    shape = quarters[0].shape
    groups = jnp.stack(quarters).reshape((n // cap, cap) + shape[1:])
    mine = holders(me, by_source)
    at = jnp.argmax(mine[None, :] == jnp.arange(peers, dtype=I32)[:, None], axis=1)
    got = lax.all_to_all(jnp.take(groups, at, axis=0), "dp", split_axis=0, concat_axis=0, tiled=True)
    slots, here = held(me, by_source)
    sources = jnp.argsort(jnp.logical_not(here), stable=True)[: n // cap]
    parts = jnp.take(got, sources, axis=0).reshape((4,) + shape)
    return [parts[i] for i in range(4)] + [jnp.take(slots, sources, axis=0).reshape(n)]


def sets_of_turns(peers):
    sets = [t for t in itertools.combinations(range(peers), 4) if {1, peers - 1} <= set(t)]
    table = [len(sets)] * (1 << peers)
    for i, turns in enumerate(sets):
        table[sum(1 << t for t in turns)] = i
    return sets, table


def tie(x, *after):
    return lax.optimization_barrier((x, *after))[0]


def on_device(embeddings, lengths, parent_slot, centroids):
    peers = lax.axis_size("dp")
    me = lax.axis_index("dp").astype(I32)
    core = (lax.axis_index("grp") & 1).astype(I32)
    me1, core1 = me.reshape(1), core.reshape(1)
    fast = peers == 8
    slots, perm = sort_parents(me1, parent_slot, peers)
    keep_a, send_a, keep_b, send_b, cents, even = split_blocks(core1, perm, embeddings, centroids)
    if fast:
        pair = jnp.concatenate([slots, swapped(slots, 1)], axis=0)
        send_a, send_b = tie(send_a, pair), tie(send_b, pair)
        rows = [pair] + [swapped(pair, step) for step in (2, 4, 6)]

    emb = [(keep_a, across(send_a, 1)), (keep_b, across(send_b, 1))]
    count, block, _ = keep_a.shape
    norms = row_facts(norms_kernel, count, block, [], [*emb[0], *emb[1]], "row_norms")

    def live_rows(*after):
        late = [tie(core1, *after), perm, lengths]
        return row_facts(lambda *refs: live_kernel(block, *refs), count, block, late, [], "live_rows")


    def first(chunk, own, *after):
        mates = [across(x, 1) for x in own]
        return first_pass(even, own, mates, tie(norms[chunk], *after), emb[chunk], chunk == 0)

    def second(chunk, lives, part, got, cur):
        cur, part, rows = second_pass(lives[chunk], part, got, cur, emb[chunk])
        return part, rows, cur

    def last(chunk, lives, part, got, rows, cur):
        return last_pass(lives[chunk], part, got, rows, cur, emb[chunk])

    def by_quarter(own, other):
        other = across(other, 1)
        return [jnp.where(core == 0, own, other), jnp.where(core == 0, other, own)]

    if not fast:
        by_source = lax.all_gather(slots, "dp", axis=0, tiled=True)
        quarters = fetch_any(me, by_source, centroids)
        lives, done = live_rows(), []
        for c in range(2):
            part, cur = first(c, [quarters[quarter_of(c, k)] for k in range(2)])
            part, rows, cur = second(c, lives, part, across(part, 2), cur)
            done += by_quarter(*last(c, lives, part, across(part, 2), rows, cur))
        return place_any(me, by_source, done)

    sets, table = sets_of_turns(peers)
    rows[0] = tie(rows[0], *norms)
    *packed, slot_list, branch = pack_centroids(me1, jnp.array(table, I32), rows, cents, peers)

    def in_order():
        return jnp.take(jnp.concatenate(rows), jnp.arange(peers, dtype=I32) ^ me, axis=0)

    def switch(body):
        return lax.switch(branch[0], [lambda turns=turns: body(turns) for turns in sets + [None]])

    def fetched(turns):
        return fetch_any(me, in_order(), centroids) if turns is None else fetch(turns, packed)

    own = switch(fetched)
    part_a, cur_a = first(1, own[2:])
    got_a = across(part_a, 2)
    part_b, cur_b = first(0, own[:2], part_a)
    got_b = across(part_b, 2)
    lives = live_rows(part_b)
    part_a, rows_a, cur_a = second(1, lives, part_a, got_a, tie(cur_a, part_b))
    got_a = across(part_a, 2)
    part_b, rows_b, cur_b = second(0, lives, part_b, got_b, tie(cur_b, part_a))
    got_b = across(part_b, 2)
    own_a, other_a = last(1, lives, part_a, got_a, rows_a, tie(cur_a, part_b))
    own_b, other_b = last(0, lives, part_b, got_b, rows_b, tie(cur_b, own_a))
    done_a = by_quarter(own_a, tie(other_a, got_b))
    done = by_quarter(own_b, other_b) + done_a

    def finish(turns):
        if turns is None:
            return place_any(me, in_order(), done)
        return place_centroids(slot_list, give(turns, done))

    return switch(finish)


def place_any(me, by_source, quarters):
    *parts, slot_list = give_any(me, by_source, quarters)
    return place_centroids(slot_list, parts)


def solution(mesh):
    return jax.shard_map(
        on_device,
        mesh=mesh,
        in_specs=(P("dp", None, "grp"), P("dp"), P("dp"), P("dp", None, "grp")),
        out_specs=P("dp", None, "grp"),
        check_vma=False,
    )
```
